768 devices in a mesh: blk: 96 (over y_lo, x, z), wn: 8 (over y_hi, core).
Axes of the slice: x: 4, y: 8 (y_hi: 4, y_lo: 2; y = y_hi * 2 + y_lo), z: 12, core: 2. Of those that a mesh axis runs over, the one named last changes fastest.
Arguments:
- species_molar_share: float32 [11, 128, 2, 12288], P(None, 'wn', None, 'blk'), may hold values from 0.01 to 1
- flow_speed_vector: float32 [2, 128, 2, 12288], P(None, 'wn', None, 'blk'), may hold values from -6 to 6
- thermal_level: float32 [128, 2, 12288], P('wn', None, 'blk'), may hold values from 0.5 to 2
- shear_collision_terms: float32 [11, 11], replicated, may hold values from 1 to 2
- thermal_collision_terms: float32 [11, 11], replicated, may hold values from 1 to 2
Outputs:
- final_state: float32 [14, 128, 2, 12288], P(None, 'wn', None, 'blk')
- last_residual: float32 [14, 128, 2, 12288], P(None, 'wn', None, 'blk')
The draws below stay inside these ranges and needn't reach their ends.
All inputs are finite; a program needn't handle non-finite values.
Results may differ from the reference program's by a relative error of at most 0.00005.
Values sent between devices are 32-bit elements; how exact they have to be, the bound alone decides.
No kernel may reach another device: no remote copies, remote signals or barrier semaphores. Data moves between devices by JAX's collectives and lax.ppermute only.
A program may use at most 32 MiB of HBM per device.

```python
import math
import jax
import jax.numpy as jnp
import numpy as np
from jax import lax

NSPEC = 11
DOWNWIND_SPAN = 12288
WALLWARD_SPAN = 128


def log_spread(key, extent, lower_end, upper_end):
    values = jnp.exp(jax.random.uniform(key, extent, jnp.float32, math.log(lower_end), math.log(upper_end)))
    return jnp.minimum(jnp.maximum(values, lower_end), upper_end)


def draw_thermal_level(key, part):
    key = jax.random.fold_in(key, 11)
    extent = (WALLWARD_SPAN, 2, DOWNWIND_SPAN)
    return log_spread(key, extent, 0.5, 2.0)


def draw_shear_collision_terms(key, part):
    key = jax.random.fold_in(key, 23)
    return log_spread(key, (NSPEC, NSPEC), 1.0, 2.0)


def draw_thermal_collision_terms(key, part):
    key = jax.random.fold_in(key, 37)
    return log_spread(key, (NSPEC, NSPEC), 1.0, 2.0)


def block_levels(own_key, shape, shards, smallest, largest):
    loudness = 1.0
    for axis_at, blocks in shards:
        draws = jax.random.uniform(jax.random.fold_in(jax.random.fold_in(own_key, 6), axis_at), (blocks,), jnp.float32, smallest / len(shards), largest / len(shards))
        loudness = loudness * jnp.repeat(jnp.exp(draws), shape[axis_at] // blocks).reshape((-1,) + (1,) * (len(shape) - 1 - axis_at))
    return loudness


def scatter_about(key, shape, deviation, limit, cuts=(), kind=jnp.bfloat16):
    entries = deviation * jax.random.normal(key, shape, jnp.float32)
    if cuts:
        entries = entries * block_levels(key, shape, cuts, -0.22, 0.18)
    return jnp.clip(entries, -limit, limit).astype(kind)


def setup_inputs(seed: int = 0) -> dict:
    key_of = jax.random.split(jax.random.key(seed), 6)
    return {
        "species_molar_share": jnp.clip(jnp.exp(math.log(1.0) - 4.6051702 * jax.random.uniform(key_of[0], (NSPEC, WALLWARD_SPAN, 2, DOWNWIND_SPAN), jnp.float32) ** block_levels(key_of[0], (NSPEC, WALLWARD_SPAN, 2, DOWNWIND_SPAN), ((1, 8), (3, 96)), -0.2, 0.2)), 0.01, 1.0),
        "flow_speed_vector": scatter_about(key_of[1], (2, WALLWARD_SPAN, 2, DOWNWIND_SPAN), 1.0, 6.0, ((1, 8), (3, 96)), jnp.float32),
        "thermal_level": draw_thermal_level(jax.random.fold_in(key_of[5], 71), 0),
        "shear_collision_terms": draw_shear_collision_terms(jax.random.fold_in(key_of[5], 71), 0),
        "thermal_collision_terms": draw_thermal_collision_terms(jax.random.fold_in(key_of[5], 71), 0),
    }


MASSES = np.array([28.0, 32.0, 30.0, 14.0, 16.0, 28.0, 32.0, 30.0, 14.0, 16.0, 0.00055]) / 28.0


def properties(padded, shear_collision_terms, thermal_collision_terms):
    fractions = padded[:11]
    heat = padded[13]
    denom_visc = jnp.einsum("sr,rjki->sjki", shear_collision_terms, fractions, precision=lax.Precision.HIGHEST)
    denom_cond = jnp.einsum("sr,rjki->sjki", thermal_collision_terms, fractions, precision=lax.Precision.HIGHEST)
    mixture_viscosity = heat ** 0.7 * jnp.sum(fractions * MASSES[:, None, None, None] / denom_visc, axis=0)
    conduct = heat ** 0.5 * jnp.sum(fractions / denom_cond, axis=0)
    return mixture_viscosity, conduct


def shifted(field, down, across):
    rows = field.shape[-3]
    cols = field.shape[-1]
    return field[..., 1 + down:rows - 1 + down, :, 1 + across:cols - 1 + across]


def diffuse(padded, coeff):
    center_c = shifted(coeff, 0, 0)
    center_face = shifted(padded, 0, 0)
    total = jnp.zeros_like(center_face)
    for down, across in ((1, 0), (-1, 0), (0, 1), (0, -1)):
        total = total + 0.5 * (center_c + shifted(coeff, down, across)) * (shifted(padded, down, across) - center_face)
    return total


def residual_of(padded, mixture_viscosity, conduct):
    return jnp.concatenate([diffuse(padded[:11], conduct), diffuse(padded[11:13], mixture_viscosity), diffuse(padded[13:], conduct)], axis=0)


def pad_state(state):
    rows_done = jnp.concatenate([state[:, 1:2, ::-1, :], state, state[:, -1:, :, :]], axis=1)
    return jnp.concatenate([rows_done[..., :1], rows_done, rows_done[:, :, ::-1, -1:]], axis=3)


def evaluate(state, shear_collision_terms, thermal_collision_terms):
    padded = pad_state(state)
    mixture_viscosity, conduct = properties(padded, shear_collision_terms, thermal_collision_terms)
    return residual_of(padded, mixture_viscosity, conduct)


def reference(species_molar_share, flow_speed_vector, thermal_level, shear_collision_terms, thermal_collision_terms):
    step = 0.16
    first_position = jnp.concatenate([species_molar_share, flow_speed_vector, thermal_level[None]], axis=0)
    first = first_position + step * evaluate(first_position, shear_collision_terms, thermal_collision_terms)
    second = 0.75 * first_position + 0.25 * (first + step * evaluate(first, shear_collision_terms, thermal_collision_terms))
    last_residual = evaluate(second, shear_collision_terms, thermal_collision_terms)
    final_state = first_position / 3.0 + 2.0 / 3.0 * (second + step * last_residual)
    return final_state, last_residual
```

```python
import jax
import jax.numpy as jnp
import numpy as np
from jax import lax
from jax.experimental import pallas as pl
from jax.experimental.pallas import tpu as pltpu
from jax.sharding import PartitionSpec as P

MASSES = [28.0, 32.0, 30.0, 14.0, 16.0, 28.0, 32.0, 30.0, 14.0, 16.0, 0.00055]
STEP = 0.16
WN = 8
BLK = 96
RUN = 12
OWN = 32
ROWS = 48
LANES = 128
CHUNK = 24


def iota(shape, dim):
    return lax.broadcasted_iota(jnp.int32, shape, dim)


def set_ghost_rows(state, wn):
    sub = iota((8, LANES), 0)
    low, high = wn == 0, wn == WN - 1
    for v in range(14):
        first = state[v, 0:8]
        last = state[v, 24:32]
        above = state[v, 32:40]
        below = state[v, 40:48]
        state[v, 32:40] = jnp.where(high & (sub < 2), pltpu.roll(last, 2, 0), above)
        cut = jnp.where(sub == 6, pltpu.roll(first, 3, 0), pltpu.roll(first, 5, 0))
        state[v, 40:48] = jnp.where(low & (sub >= 6), cut, below)


def coefficients(state, coeff, shear, thermal):
    for c in range(ROWS // CHUNK):
        rows = pl.ds(c * CHUNK, CHUNK)
        x = [state[r, rows] for r in range(11)]
        logs = jnp.log(state[13, rows])
        visc = cond = None
        for s in range(11):
            dv = shear[s, 0] * x[0]
            dc = thermal[s, 0] * x[0]
            for r in range(1, 11):
                dv = dv + shear[s, r] * x[r]
                dc = dc + thermal[s, r] * x[r]
            tv = x[s] * np.float32(MASSES[s] / 28.0) / dv
            tc = x[s] / dc
            visc = tv if visc is None else visc + tv
            cond = tc if cond is None else cond + tc
        coeff[0, rows] = jnp.exp(0.7 * logs) * (0.5 * visc)
        coeff[1, rows] = jnp.exp(0.5 * logs) * (0.5 * cond)


def faces(coeff):
    out = []
    for k in (coeff[1], coeff[0]):
        out.append((k + pltpu.roll(k, ROWS - 2, 0), k + pltpu.roll(k, LANES - 1, 1)))
    return out


def residual(w, face):
    down, across = face
    f = down * (pltpu.roll(w, ROWS - 2, 0) - w)
    g = across * (pltpu.roll(w, LANES - 1, 1) - w)
    return (f - pltpu.roll(f, 2, 0)) + (g - pltpu.roll(g, 1, 1))


def sections(fix, w0, wa, wb, coeff, shear, thermal, emit):
    fix(w0)
    coefficients(w0, coeff, shear, thermal)
    face = faces(coeff)
    for v in range(14):
        w = w0[v]
        wa[v] = w + STEP * residual(w, face[v in (11, 12)])
    fix(wa)
    coefficients(wa, coeff, shear, thermal)
    face = faces(coeff)
    for v in range(14):
        w = wa[v]
        wb[v] = 0.75 * w0[v] + 0.25 * (w + STEP * residual(w, face[v in (11, 12)]))
    fix(wb)
    coefficients(wb, coeff, shear, thermal)
    face = faces(coeff)
    for v in range(14):
        w = wb[v]
        last = residual(w, face[v in (11, 12)])
        final = w0[v] * np.float32(1.0 / 3.0) + np.float32(2.0 / 3.0) * (w + STEP * last)
        emit(v, final[:OWN], last[:OWN])


def pack_columns(rows):
    missing = -rows.shape[0] % LANES
    if missing:
        rows = jnp.concatenate([rows, jnp.zeros((missing, LANES), jnp.float32)], axis=0)
    left, right = [], []
    for t in range(rows.shape[0] // LANES):
        turned = rows[t * LANES : (t + 1) * LANES].T
        left.append(turned[:8])
        right.append(turned[120:])
    return left, right


def load_kernel(species, flow, heat, block, left, right, corner, top, bottom):
    block[0:11] = species[...]
    block[11:13] = flow[...]
    block[13:14] = heat[...]
    lefts, rights = pack_columns(block[...].reshape(14 * OWN, LANES))
    for t in range(4):
        left[t] = lefts[t]
        right[t] = rights[t]
    low, high = block[:, 0:8], block[:, 24:32]
    bottom[...] = low
    top[...] = high
    _, rights = pack_columns(jnp.concatenate([low, high], axis=1).reshape(14 * 16, LANES))
    for t in range(2):
        corner[t] = rights[t]


def edge_kernel(above, below, left, right, pair, other):
    even = lax.axis_index("blk") % 2 == 0
    halo = jnp.concatenate([above[...], below[...]], axis=1).reshape(14 * 16, LANES)
    lefts, rights = pack_columns(halo)
    for t in range(6):
        lo = left[t] if t < 4 else lefts[t - 4]
        hi = right[t] if t < 4 else rights[t - 4]
        pair[t] = jnp.where(even, hi, lo)
        pair[t + 6] = lo
        other[t] = jnp.where(even, lo, hi)


def gather_rows(block, above, below, w0):
    for v in range(14):
        w0[v, 0:32] = block[v]
        w0[v, 32:40] = above[v]
        w0[v, 40:48] = below[v]


def main_kernel(block, above, below, shear, thermal, final, last, w0, wa, wb, coeff):
    wn = lax.axis_index("wn")
    gather_rows(block, above, below, w0)

    def emit(v, f, r):
        final[v] = f
        last[v] = r

    sections(lambda ref: set_ghost_rows(ref, wn), w0, wa, wb, coeff, shear, thermal, emit)


def strip_kernel(
    block, above, below, pair, other, relay, wrap, wrap_up, wrap_down, shear, thermal, main_final, main_last,
    final, last, w0, wa, wb, coeff,
):
    wn = lax.axis_index("wn")
    blk = lax.axis_index("blk")
    even = blk % 2 == 0
    place = blk % RUN
    lane = iota((ROWS, LANES), 1)
    gather_rows(block, above, below, w0)
    lane8 = iota((8, LANES), 1)
    tiles = []
    for t in range(6):
        if t < 4:
            from_wrap = wrap[t]
        else:
            from_wrap = jnp.where(lane8 % 16 < 8, wrap_up[t - 4], wrap_down[t - 4])
        lo = jnp.where(place == 0, from_wrap, jnp.where(even, other[t], pair[t]))
        hi = jnp.where(place == RUN - 1, relay[t], jnp.where(even, pair[t], other[t]))
        full = jnp.concatenate([hi, lo, jnp.zeros((112, LANES), jnp.float32)], axis=0)
        tiles.append(full.T)
    for v in range(14):
        own = w0[v]
        q, h = v % 4, v % 8
        side = jnp.concatenate([tiles[v // 4][q * 32 : q * 32 + 32], tiles[4 + v // 8][h * 16 : h * 16 + 16]], axis=0)
        w0[v] = jnp.where(lane < 16, side, jnp.where(lane < 72, pltpu.roll(own, 16, 1), own))

    first, nose = blk == 0, blk == BLK - 1
    even_row = iota((ROWS, LANES), 0) % 2 == 0

    def fix(ref):
        set_ghost_rows(ref, wn)

        @pl.when(first)
        def _():
            for v in range(14):
                w = ref[v]
                ref[v] = jnp.where(lane == 15, pltpu.roll(w, LANES - 1, 1), w)

        @pl.when(nose)
        def _():
            for v in range(14):
                w = ref[v]
                moved = pltpu.roll(w, 1, 1)
                swapped = jnp.where(even_row, pltpu.roll(moved, ROWS - 1, 0), pltpu.roll(moved, 1, 0))
                ref[v] = jnp.where(lane == 0, swapped, w)

    lane_own = iota((OWN, LANES), 1)

    def emit(v, f, r):
        for out, new, old in ((final, f, main_final), (last, r, main_last)):
            out[v] = jnp.where(lane_own < 3, pltpu.roll(new, LANES - 16, 1), jnp.where(lane_own >= 125, new, old[v]))

    sections(fix, w0, wa, wb, coeff, shear, thermal, emit)


VMEM = pl.BlockSpec(memory_space=pltpu.VMEM)
SMEM = pl.BlockSpec(memory_space=pltpu.SMEM)
SCRATCH = [pltpu.VMEM((14, ROWS, LANES), jnp.float32)] * 3 + [pltpu.VMEM((2, ROWS, LANES), jnp.float32)]
PARAMS = pltpu.CompilerParams(vmem_limit_bytes=12 * 1024 * 1024)


def f32(*shape):
    return jax.ShapeDtypeStruct(shape, jnp.float32)


def call(kernel, outs, ins, scratch=()):
    return pl.pallas_call(
        kernel, out_shape=outs, in_specs=ins, out_specs=tuple(VMEM for _ in outs), scratch_shapes=scratch, compiler_params=PARAMS
    )


def at(blk, wn):
    return blk * WN + wn


def send(x, pairs):
    return lax.ppermute(x, ("blk", "wn"), pairs)


def wrap_pairs(shift):
    return [
        (at(b, w), at(b + 1, w + shift))
        for b in range(RUN - 1, BLK - 1, RUN)
        for w in range(WN)
        if 0 <= w + shift < WN
    ]


PAIRS = [(at(b + i, w), at(b + 1 - i, w)) for b in range(0, BLK, 2) for w in range(WN) for i in range(2)]
OTHERS = [
    (at(b + i, w), at(b + 1 - i, w)) for b in range(1, BLK - 1, 2) if (b + 1) % RUN for w in range(WN) for i in range(2)
]
RELAY = [(at(b + 1, w), at(b - 1, w)) for b in range(RUN, BLK, RUN) for w in range(WN)]
UP = [(at(b, w), at(b, w + 1)) for b in range(BLK) for w in range(WN - 1)]
DOWN = [(target, source) for source, target in UP]


def local(species, flow, heat, shear, thermal):
    species = species.reshape(11, OWN, LANES)
    flow = flow.reshape(2, OWN, LANES)
    heat = heat.reshape(1, OWN, LANES)
    block, left, right, corner, top, bottom = call(
        load_kernel,
        (f32(14, OWN, LANES), f32(4, 8, LANES), f32(4, 8, LANES), f32(2, 8, LANES), f32(14, 8, LANES), f32(14, 8, LANES)),
        [VMEM] * 3,
    )(species, flow, heat)
    wrap_up = send(corner, wrap_pairs(-1))
    wrap = send(right, wrap_pairs(0))
    wrap_down = send(corner, wrap_pairs(1))
    above = send(bottom, DOWN)
    below = send(top, UP)
    pair, other = call(edge_kernel, (f32(12, 8, LANES), f32(6, 8, LANES)), [VMEM] * 4)(above, below, left, right)
    got_pair = send(pair, PAIRS)
    got_other = send(other, OTHERS)
    relay = send(got_pair[6:], RELAY)
    out = f32(14, OWN, LANES)
    main_final, main_last = call(main_kernel, (out, out), [VMEM] * 3 + [SMEM] * 2, SCRATCH)(block, above, below, shear, thermal)
    final, last = call(strip_kernel, (out, out), [VMEM] * 9 + [SMEM] * 2 + [VMEM] * 2, SCRATCH)(
        block, above, below, got_pair, got_other, relay, wrap, wrap_up, wrap_down, shear, thermal, main_final, main_last
    )
    return final.reshape(14, 16, 2, LANES), last.reshape(14, 16, 2, LANES)


def solution(mesh):
    return jax.shard_map(
        local,
        mesh=mesh,
        in_specs=(P(None, "wn", None, "blk"), P(None, "wn", None, "blk"), P("wn", None, "blk"), P(), P()),
        out_specs=(P(None, "wn", None, "blk"), P(None, "wn", None, "blk")),
        check_vma=False,
    )
```

```python
import jax
import jax.numpy as jnp
import numpy as np
from jax import lax
from jax.experimental import pallas as pl
from jax.experimental.pallas import tpu as pltpu
from jax.sharding import PartitionSpec as P

MASSES = [28.0, 32.0, 30.0, 14.0, 16.0, 28.0, 32.0, 30.0, 14.0, 16.0, 0.00055]
STEP = 0.16
WN = 8
BLK = 96
RUN = 12
OWN = 32
ROWS = 48
LANES = 128
CHUNK = 24


def iota(shape, dim):
    return lax.broadcasted_iota(jnp.int32, shape, dim)


def set_ghost_rows(state, wn):
    sub = iota((8, LANES), 0)
    low, high = wn == 0, wn == WN - 1
    for v in range(14):
        first = state[v, 0:8]
        last = state[v, 24:32]
        above = state[v, 32:40]
        below = state[v, 40:48]
        state[v, 32:40] = jnp.where(high & (sub < 2), pltpu.roll(last, 2, 0), above)
        cut = jnp.where(sub == 6, pltpu.roll(first, 3, 0), pltpu.roll(first, 5, 0))
        state[v, 40:48] = jnp.where(low & (sub >= 6), cut, below)


def coefficients(state, coeff, shear, thermal):
    for c in range(ROWS // CHUNK):
        rows = pl.ds(c * CHUNK, CHUNK)
        x = [state[r, rows] for r in range(11)]
        logs = jnp.log(state[13, rows])
        visc = cond = None
        for s in range(11):
            dv = shear[s, 0] * x[0]
            dc = thermal[s, 0] * x[0]
            for r in range(1, 11):
                dv = dv + shear[s, r] * x[r]
                dc = dc + thermal[s, r] * x[r]
            tv = x[s] * np.float32(MASSES[s] / 28.0) / dv
            tc = x[s] / dc
            visc = tv if visc is None else visc + tv
            cond = tc if cond is None else cond + tc
        coeff[0, rows] = jnp.exp(0.7 * logs) * (0.5 * visc)
        coeff[1, rows] = jnp.exp(0.5 * logs) * (0.5 * cond)


def faces(coeff):
    out = []
    for k in (coeff[1], coeff[0]):
        out.append((k + pltpu.roll(k, ROWS - 2, 0), k + pltpu.roll(k, LANES - 1, 1)))
    return out


def residual(w, face):
    down, across = face
    f = down * (pltpu.roll(w, ROWS - 2, 0) - w)
    g = across * (pltpu.roll(w, LANES - 1, 1) - w)
    return (f - pltpu.roll(f, 2, 0)) + (g - pltpu.roll(g, 1, 1))


def sections(fix, w0, wa, wb, coeff, shear, thermal, emit):
    fix(w0)
    coefficients(w0, coeff, shear, thermal)
    face = faces(coeff)
    for v in range(14):
        w = w0[v]
        wa[v] = w + STEP * residual(w, face[v in (11, 12)])
    fix(wa)
    coefficients(wa, coeff, shear, thermal)
    face = faces(coeff)
    for v in range(14):
        w = wa[v]
        wb[v] = 0.75 * w0[v] + 0.25 * (w + STEP * residual(w, face[v in (11, 12)]))
    fix(wb)
    coefficients(wb, coeff, shear, thermal)
    face = faces(coeff)
    for v in range(14):
        w = wb[v]
        last = residual(w, face[v in (11, 12)])
        final = w0[v] * np.float32(1.0 / 3.0) + np.float32(2.0 / 3.0) * (w + STEP * last)
        emit(v, final[:OWN], last[:OWN])


def pack_columns(rows):
    missing = -rows.shape[0] % LANES
    if missing:
        rows = jnp.concatenate([rows, jnp.zeros((missing, LANES), jnp.float32)], axis=0)
    left, right = [], []
    for t in range(rows.shape[0] // LANES):
        turned = rows[t * LANES : (t + 1) * LANES].T
        left.append(turned[:8])
        right.append(turned[120:])
    return left, right


def load_kernel(species, flow, heat, block, right, corner, sems):
    copies = [
        pltpu.make_async_copy(source, block.at[pl.ds(low, count)], sems.at[i])
        for i, (source, low, count) in enumerate(((species, 0, 11), (flow, 11, 2), (heat, 13, 1)))
    ]
    for copy in copies:
        copy.start()
    for copy in copies:
        copy.wait()
    _, rights = pack_columns(block[...].reshape(14 * OWN, LANES))
    for t in range(4):
        right[t] = rights[t]
    low, high = block[:, 0:8], block[:, 24:32]
    _, rights = pack_columns(jnp.concatenate([low, high], axis=1).reshape(14 * 16, LANES))
    for t in range(2):
        corner[t] = rights[t]


def second_rows_kernel(block, second):
    even = lax.axis_index("wn") % 2 == 0
    second[...] = jnp.where(even, block[:, 0:8], block[:, 24:32])


def first_rows_kernel(block, after, first):
    even = lax.axis_index("wn") % 2 == 0
    for v in range(14):
        first[pl.ds(6 * v, 6)] = jnp.where(even, block[v, 26:32], block[v, 0:6])


def pass_kernel(value, after, out):
    out[...] = value[...]


def halo_of(first, second):
    even = lax.axis_index("wn") % 2 == 0
    zeros = jnp.zeros((2, LANES), jnp.float32)
    two = second[...]
    one = [first[pl.ds(6 * v, 6)] for v in range(14)]
    above = jnp.stack([jnp.concatenate([x, zeros], axis=0) for x in one])
    below = jnp.stack([jnp.concatenate([zeros, x], axis=0) for x in one])
    return jnp.concatenate([jnp.where(even, above, two), jnp.where(even, two, below)], axis=1)


def columns_of(block, halo):
    lefts, rights = pack_columns(block[...].reshape(14 * OWN, LANES))
    lefts_halo, rights_halo = pack_columns(halo.reshape(14 * 16, LANES))
    return lefts + lefts_halo, rights + rights_halo


def early_columns_kernel(first, second, block, halo, pair, lows, highs):
    even = lax.axis_index("blk") % 2 == 0
    halo[...] = halo_of(first, second)
    lefts, rights = columns_of(block, halo[...])
    for t in range(6):
        three = pl.ds(3 * t, 3)
        pair[three] = jnp.where(even, rights[t][5:8], lefts[t][0:3])
        lows[three] = lefts[t][0:3]
        highs[three] = rights[t][5:8]


def late_columns_kernel(first, second, block, halo, lows, highs):
    halo[...] = halo_of(first, second)
    lefts, rights = columns_of(block, halo[...])
    for t in range(6):
        three = pl.ds(3 * t, 3)
        highs[three] = rights[t][5:8]
        lows[three] = lefts[t][0:3]


def keep_kernel(early_lows, early_highs, lows, highs):
    lows[...] = early_lows[...]
    highs[...] = early_highs[...]


def gather_rows(block, halo, w0):
    for v in range(14):
        w0[v, 0:OWN] = block[v]
        w0[v, OWN:ROWS] = halo[v]


def main_sections(block, halo, shear, thermal, final, last, w0, wa, wb, coeff):
    wn = lax.axis_index("wn")
    if halo is not None:
        gather_rows(block, halo, w0)

    def emit(v, f, r):
        final[v] = f
        last[v] = r

    sections(lambda ref: set_ghost_rows(ref, wn), w0, wa, wb, coeff, shear, thermal, emit)


def early_main_kernel(block, halo, shear, thermal, final, last, w0, wa, wb, coeff):
    main_sections(block, halo, shear, thermal, final, last, w0, wa, wb, coeff)


def idle_kernel(*refs):
    pass


def last_kernel(
    block, early_halo, late_halo, early_pair, left, right, relay, wrap, wrap_up, wrap_down, shear, thermal, main_final, main_last,
    final, last, w0, wa, wb, coeff, sems,
):
    wn = lax.axis_index("wn")
    blk = lax.axis_index("blk")
    place = blk % RUN

    halo_rows = w0.at[:, pl.ds(OWN, 16)]
    mains = [pltpu.make_async_copy(a, b, sems.at[i]) for i, (a, b) in enumerate(((main_final, final), (main_last, last)))]

    @pl.when(place == 0)
    def _():
        for copy in mains:
            copy.start()

    for known, halo in ((place <= 1, early_halo), (place > 1, late_halo)):

        @pl.when(known)
        def _():
            copy = pltpu.make_async_copy(halo, halo_rows, sems.at[2])
            copy.start()
            for v in range(14):
                w0[v, 0:OWN] = block[v]
            copy.wait()

    @pl.when(place != 0)
    def _():
        main_sections(block, None, shear, thermal, final, last, w0, wa, wb, coeff)

    lane = iota((ROWS, LANES), 1)
    for v in range(14):
        w0[v, 0:OWN] = block[v]
    lane3 = iota((3, LANES), 1)
    tiles = []
    for t in range(6):
        three = pl.ds(3 * t, 3)
        if t < 4:
            from_wrap = wrap[t, 5:8]
        else:
            from_wrap = jnp.where(lane3 % 16 < 8, wrap_up[t - 4, 5:8], wrap_down[t - 4, 5:8])
        lo = jnp.where(place == 0, from_wrap, jnp.where(place == 1, early_pair[three], left[three]))
        hi = jnp.where(place == RUN - 1, relay[three], jnp.where(place == 0, early_pair[three], right[three]))
        full = jnp.concatenate([hi, jnp.zeros((10, LANES), jnp.float32), lo, jnp.zeros((112, LANES), jnp.float32)], axis=0)
        tiles.append(full.T)
    for v in range(14):
        own = w0[v]
        q, h = v % 4, v % 8
        side = jnp.concatenate([tiles[v // 4][q * 32 : q * 32 + 32], tiles[4 + v // 8][h * 16 : h * 16 + 16]], axis=0)
        w0[v] = jnp.where(lane < 16, side, jnp.where(lane < 72, pltpu.roll(own, 16, 1), own))

    first, nose = blk == 0, blk == BLK - 1
    even_row = iota((ROWS, LANES), 0) % 2 == 0

    def fix(ref):
        set_ghost_rows(ref, wn)

        @pl.when(first)
        def _():
            for v in range(14):
                w = ref[v]
                ref[v] = jnp.where(lane == 15, pltpu.roll(w, LANES - 1, 1), w)

        @pl.when(nose)
        def _():
            for v in range(14):
                w = ref[v]
                moved = pltpu.roll(w, 1, 1)
                swapped = jnp.where(even_row, pltpu.roll(moved, ROWS - 1, 0), pltpu.roll(moved, 1, 0))
                ref[v] = jnp.where(lane == 0, swapped, w)

    lane_own = iota((OWN, LANES), 1)

    def emit(v, f, r):
        if v == 0:

            @pl.when(place == 0)
            def _():
                for copy in mains:
                    copy.wait()

        for out, new in ((final, f), (last, r)):
            out[v] = jnp.where(lane_own < 3, pltpu.roll(new, LANES - 16, 1), jnp.where(lane_own >= 125, new, out[v]))

    sections(fix, w0, wa, wb, coeff, shear, thermal, emit)


VMEM = pl.BlockSpec(memory_space=pltpu.VMEM)
HBM = pl.BlockSpec(memory_space=pltpu.HBM)
ANY = pl.BlockSpec(memory_space=pl.ANY)
SMEM = pl.BlockSpec(memory_space=pltpu.SMEM)
SCRATCH = [pltpu.VMEM((14, ROWS, LANES), jnp.float32)] * 3 + [pltpu.VMEM((2, ROWS, LANES), jnp.float32)]
PARAMS = pltpu.CompilerParams(vmem_limit_bytes=12 * 1024 * 1024)


def f32(*shape):
    return jax.ShapeDtypeStruct(shape, jnp.float32)


def call(kernel, outs, ins, scratch=()):
    return pl.pallas_call(
        kernel, out_shape=outs, in_specs=ins, out_specs=tuple(VMEM for _ in outs), scratch_shapes=scratch, compiler_params=PARAMS,
        cost_estimate=pl.CostEstimate(flops=1, bytes_accessed=1, transcendentals=0),
    )


def at(blk, wn):
    return blk * WN + wn


def send(x, pairs):
    return lax.ppermute(x, ("blk", "wn"), pairs)


def wrap_pairs(shift):
    return [
        (at(b, w), at(b + 1, w + shift))
        for b in range(RUN - 1, BLK - 1, RUN)
        for w in range(WN)
        if 0 <= w + shift < WN
    ]


def swap(pairs):
    return pairs + [(target, source) for source, target in pairs]


def rows_pairs(start, early):
    return swap([
        (at(b, w), at(b, w + 1)) for b in range(BLK) if (b % RUN < 2 if early else b % RUN > 1) for w in range(start, WN - 1, 2)
    ])


def columns_pairs(places):
    return [(at(b, w), at(b + 1, w)) for b in range(BLK - 1) if b % RUN in places for w in range(WN)]


FIRST = swap(columns_pairs((0,)))
FORWARD = columns_pairs(range(1, RUN - 1))
BACKWARD = [(target, source) for source, target in FORWARD]
RELAY = [(at(b, w), at(b - 1, w)) for b in range(RUN, BLK, RUN) for w in range(WN)]


def idle(*outs):
    return tuple(pl.pallas_call(idle_kernel, out_shape=outs, out_specs=tuple(HBM for _ in outs))())


def in_hbm(x):
    return pltpu.with_memory_space_constraint(x, pltpu.HBM)


def local(species, flow, heat, shear, thermal):
    strips = f32(18, LANES)
    rows = f32(14, 8, LANES)
    halo_shape = f32(14, 16, LANES)
    out = f32(14, OWN, LANES)
    place = lax.axis_index("blk") % RUN
    shear, thermal = in_hbm(shear), in_hbm(thermal)
    block, right, corner = call(
        load_kernel,
        (out, f32(4, 8, LANES), f32(2, 8, LANES)),
        [HBM] * 3,
        [pltpu.SemaphoreType.DMA((3,))],
    )(in_hbm(species.reshape(11, OWN, LANES)), in_hbm(flow.reshape(2, OWN, LANES)), in_hbm(heat.reshape(1, OWN, LANES)))
    wrap_up = send(corner, wrap_pairs(-1))
    wrap = send(right, wrap_pairs(0))
    wrap_down = send(corner, wrap_pairs(1))

    def exchange_rows(block, early):
        second = call(second_rows_kernel, (rows,), [VMEM])(block)[0]
        second = send(second, rows_pairs(1, early))
        first = call(first_rows_kernel, (f32(84, LANES),), [VMEM, ANY])(block, block if early else second)[0]
        first = send(first, rows_pairs(0, early))
        return first, second

    def early(block, shear, thermal):
        first, second = exchange_rows(block, True)
        halo, pair, lows, highs = call(early_columns_kernel, (halo_shape, strips, strips, strips), [VMEM] * 3)(first, second, block)
        pair = send(pair, FIRST)
        final, last = lax.cond(place == 0, main, no_main, block, halo, shear, thermal)
        return halo, pair, lows, highs, final, last

    def not_early(block, shear, thermal):
        return idle(halo_shape, strips, strips, strips, out, out)

    def main(block, halo, shear, thermal):
        return tuple(call(early_main_kernel, (out, out), [VMEM] * 2 + [SMEM] * 2, SCRATCH)(block, halo, shear, thermal))

    def no_main(block, halo, shear, thermal):
        return idle(out, out)

    def edges(block, lows, highs):
        first, second = exchange_rows(block, False)
        return tuple(call(late_columns_kernel, (halo_shape, strips, strips), [VMEM] * 3)(first, second, block))

    def known_edges(block, lows, highs):
        return (*idle(halo_shape), *call(keep_kernel, (strips, strips), [VMEM] * 2)(lows, highs))

    def late(block, lows, highs):
        halo, lows, highs = lax.cond(place > 1, edges, known_edges, block, lows, highs)
        left = send(highs, FORWARD)
        lows = call(pass_kernel, (strips,), [VMEM, ANY])(lows, left)[0]
        right = send(lows, BACKWARD)
        return halo, left, right

    def not_late(block, lows, highs):
        return idle(halo_shape, strips, strips)

    def neighbours(block, shear, thermal):
        early_halo, early_pair, lows, highs, main_final, main_last = lax.cond(place <= 1, early, not_early, block, shear, thermal)

        def rest(block, lows, highs):
            relay = send(lows, RELAY)
            halo, left, right = lax.cond(place > 0, late, not_late, block, lows, highs)
            return halo, left, right, relay

        def no_rest(block, lows, highs):
            return idle(halo_shape, strips, strips, strips)

        halo, left, right, relay = lax.cond(
            at(lax.axis_index("blk"), lax.axis_index("wn")) < 2 * at(BLK, WN), rest, no_rest, block, lows, highs
        )
        return early_halo, halo, early_pair, left, right, relay, main_final, main_last

    def none(block, shear, thermal):
        return idle(halo_shape, halo_shape, strips, strips, strips, strips, out, out)

    early_halo, halo, early_pair, left, right, relay, main_final, main_last = lax.cond(
        at(lax.axis_index("blk"), lax.axis_index("wn")) < at(BLK, WN), neighbours, none, block, shear, thermal
    )
    final, last = call(
        last_kernel, (out, out), [VMEM] + [HBM] * 2 + [VMEM] * 7 + [SMEM] * 2 + [HBM] * 2, SCRATCH + [pltpu.SemaphoreType.DMA((3,))]
    )(
        block, early_halo, halo, early_pair, left, right, relay, wrap, wrap_up, wrap_down, shear, thermal, main_final, main_last
    )
    return final.reshape(14, 16, 2, LANES), last.reshape(14, 16, 2, LANES)


def solution(mesh):
    return jax.shard_map(
        local,
        mesh=mesh,
        in_specs=(P(None, "wn", None, "blk"), P(None, "wn", None, "blk"), P("wn", None, "blk"), P(), P()),
        out_specs=(P(None, "wn", None, "blk"), P(None, "wn", None, "blk")),
        check_vma=False,
    )
```

```python
import jax
import jax.numpy as jnp
import numpy as np
from jax import lax
from jax.experimental import pallas as pl
from jax.experimental.pallas import tpu as pltpu
from jax.sharding import PartitionSpec as P

MASSES = [28.0, 32.0, 30.0, 14.0, 16.0, 28.0, 32.0, 30.0, 14.0, 16.0, 0.00055]
STEP = 0.16
WN = 8
BLK = 96
RUN = 12
OWN = 32
ROWS = 48
LANES = 128
CHUNK = 24


def iota(shape, dim):
    return lax.broadcasted_iota(jnp.int32, shape, dim)


def set_ghost_rows(state, wn):
    sub = iota((8, LANES), 0)
    low, high = wn == 0, wn == WN - 1
    for v in range(14):
        first = state[v, 0:8]
        last = state[v, 24:32]
        above = state[v, 32:40]
        below = state[v, 40:48]
        state[v, 32:40] = jnp.where(high & (sub < 2), pltpu.roll(last, 2, 0), above)
        cut = jnp.where(sub == 6, pltpu.roll(first, 3, 0), pltpu.roll(first, 5, 0))
        state[v, 40:48] = jnp.where(low & (sub >= 6), cut, below)


def coefficients(state, coeff, shear, thermal):
    for c in range(ROWS // CHUNK):
        rows = pl.ds(c * CHUNK, CHUNK)
        x = [state[r, rows] for r in range(11)]
        logs = jnp.log(state[13, rows])
        visc = cond = None
        for s in range(11):
            dv = shear[s, 0] * x[0]
            dc = thermal[s, 0] * x[0]
            for r in range(1, 11):
                dv = dv + shear[s, r] * x[r]
                dc = dc + thermal[s, r] * x[r]
            tv = x[s] * np.float32(MASSES[s] / 28.0) / dv
            tc = x[s] / dc
            visc = tv if visc is None else visc + tv
            cond = tc if cond is None else cond + tc
        coeff[0, rows] = jnp.exp(0.7 * logs) * (0.5 * visc)
        coeff[1, rows] = jnp.exp(0.5 * logs) * (0.5 * cond)


def faces(coeff):
    out = []
    for k in (coeff[1], coeff[0]):
        out.append((k + pltpu.roll(k, ROWS - 2, 0), k + pltpu.roll(k, LANES - 1, 1)))
    return out


def residual(w, face):
    down, across = face
    f = down * (pltpu.roll(w, ROWS - 2, 0) - w)
    g = across * (pltpu.roll(w, LANES - 1, 1) - w)
    return (f - pltpu.roll(f, 2, 0)) + (g - pltpu.roll(g, 1, 1))


def sections(fix, w0, wa, wb, coeff, shear, thermal, emit):
    fix(w0)
    coefficients(w0, coeff, shear, thermal)
    face = faces(coeff)
    for v in range(14):
        w = w0[v]
        wa[v] = w + STEP * residual(w, face[v in (11, 12)])
    fix(wa)
    coefficients(wa, coeff, shear, thermal)
    face = faces(coeff)
    for v in range(14):
        w = wa[v]
        wb[v] = 0.75 * w0[v] + 0.25 * (w + STEP * residual(w, face[v in (11, 12)]))
    fix(wb)
    coefficients(wb, coeff, shear, thermal)
    face = faces(coeff)
    for v in range(14):
        w = wb[v]
        last = residual(w, face[v in (11, 12)])
        final = w0[v] * np.float32(1.0 / 3.0) + np.float32(2.0 / 3.0) * (w + STEP * last)
        emit(v, final[:OWN], last[:OWN])


def pack_columns(rows):
    missing = -rows.shape[0] % LANES
    if missing:
        rows = jnp.concatenate([rows, jnp.zeros((missing, LANES), jnp.float32)], axis=0)
    left, right = [], []
    for t in range(rows.shape[0] // LANES):
        turned = rows[t * LANES : (t + 1) * LANES].T
        left.append(turned[:8])
        right.append(turned[120:])
    return left, right


def load_kernel(species, flow, heat, block, right, corner, sems):
    copies = [
        pltpu.make_async_copy(source, block.at[pl.ds(low, count)], sems.at[i])
        for i, (source, low, count) in enumerate(((species, 0, 11), (flow, 11, 2), (heat, 13, 1)))
    ]
    for copy in copies:
        copy.start()
    for copy in copies:
        copy.wait()
    _, rights = pack_columns(block[...].reshape(14 * OWN, LANES))
    for t in range(4):
        right[t] = rights[t]
    low, high = block[:, 0:8], block[:, 24:32]
    _, rights = pack_columns(jnp.concatenate([low, high], axis=1).reshape(14 * 16, LANES))
    for t in range(3):
        corner[t] = rights[t % 2]


def second_rows_kernel(block, second):
    even = lax.axis_index("wn") % 2 == 0
    second[...] = jnp.where(even, block[:, 0:8], block[:, 24:32])


def first_rows_kernel(block, after, first):
    even = lax.axis_index("wn") % 2 == 0
    for v in range(14):
        first[pl.ds(6 * v, 6)] = jnp.where(even, block[v, 26:32], block[v, 0:6])


def pass_kernel(value, after, out):
    out[...] = value[...]


def halo_of(first, second):
    even = lax.axis_index("wn") % 2 == 0
    zeros = jnp.zeros((2, LANES), jnp.float32)
    two = second[...]
    one = [first[pl.ds(6 * v, 6)] for v in range(14)]
    above = jnp.stack([jnp.concatenate([x, zeros], axis=0) for x in one])
    below = jnp.stack([jnp.concatenate([zeros, x], axis=0) for x in one])
    return jnp.concatenate([jnp.where(even, above, two), jnp.where(even, two, below)], axis=1)


def columns_of(block, halo):
    lefts, rights = pack_columns(block[...].reshape(14 * OWN, LANES))
    lefts_halo, rights_halo = pack_columns(halo.reshape(14 * 16, LANES))
    return lefts + lefts_halo, rights + rights_halo


def early_columns_kernel(first, second, block, halo, pair, lows, highs):
    even = lax.axis_index("blk") % 2 == 0
    halo[...] = halo_of(first, second)
    lefts, rights = columns_of(block, halo[...])
    for t in range(6):
        three = pl.ds(3 * t, 3)
        pair[three] = jnp.where(even, rights[t][5:8], lefts[t][0:3])
        lows[three] = lefts[t][0:3]
        highs[three] = rights[t][5:8]


def late_columns_kernel(first, second, block, halo, lows, highs):
    halo[...] = halo_of(first, second)
    lefts, rights = columns_of(block, halo[...])
    for t in range(6):
        three = pl.ds(3 * t, 3)
        highs[three] = rights[t][5:8]
        lows[three] = lefts[t][0:3]


def keep_kernel(early_lows, early_highs, lows, highs):
    lows[...] = early_lows[...]
    highs[...] = early_highs[...]


def gather_rows(block, halo, w0):
    for v in range(14):
        w0[v, 0:OWN] = block[v]
        w0[v, OWN:ROWS] = halo[v]


def main_sections(block, halo, shear, thermal, final, last, w0, wa, wb, coeff):
    wn = lax.axis_index("wn")
    if halo is not None:
        gather_rows(block, halo, w0)

    def emit(v, f, r):
        final[v] = f
        last[v] = r

    sections(lambda ref: set_ghost_rows(ref, wn), w0, wa, wb, coeff, shear, thermal, emit)


def early_main_kernel(block, halo, shear, thermal, final, last, w0, wa, wb, coeff):
    main_sections(block, halo, shear, thermal, final, last, w0, wa, wb, coeff)


def idle_kernel(*refs):
    pass


def late_main_kernel(block, early_halo, late_halo, shear, thermal, halo, final, last, w0, wa, wb, coeff, sem):
    place = lax.axis_index("blk") % RUN
    for known, source in ((place <= 1, early_halo), (place > 1, late_halo)):

        @pl.when(known)
        def _():
            copy = pltpu.make_async_copy(source, halo, sem)
            copy.start()
            copy.wait()

    @pl.when(place != 0)
    def _():
        main_sections(block, halo, shear, thermal, final, last, w0, wa, wb, coeff)


def last_kernel(
    block, halo, early_pair, left, right, relay, wrap, wrap_up, wrap_down, shear, thermal,
    early_final, early_last, late_final, late_last, final, last, w0, wa, wb, coeff, finals, lasts, in_sems, out_sems,
):
    wn = lax.axis_index("wn")
    blk = lax.axis_index("blk")
    place = blk % RUN
    mains = [pltpu.make_async_copy(a, b, in_sems.at[i]) for i, (a, b) in enumerate(((early_final, finals), (early_last, lasts)))]

    @pl.when(place == 0)
    def _():
        for copy in mains:
            copy.start()

    lane = iota((ROWS, LANES), 1)
    gather_rows(block, halo, w0)
    lane3 = iota((3, LANES), 1)
    tiles = []
    for t in range(6):
        three = pl.ds(3 * t, 3)
        if t < 4:
            from_wrap = wrap[t, 5:8]
        else:
            from_wrap = jnp.where(lane3 % 16 < 8, wrap_up[t - 4, 5:8], wrap_down[t - 4, 5:8])
        lo = jnp.where(place == 0, from_wrap, jnp.where(place == 1, early_pair[three], left[three]))
        hi = jnp.where(place == RUN - 1, relay[three], jnp.where(place == 0, early_pair[three], right[three]))
        full = jnp.concatenate([hi, jnp.zeros((10, LANES), jnp.float32), lo, jnp.zeros((112, LANES), jnp.float32)], axis=0)
        tiles.append(full.T)
    for v in range(14):
        own = w0[v]
        q, h = v % 4, v % 8
        side = jnp.concatenate([tiles[v // 4][q * 32 : q * 32 + 32], tiles[4 + v // 8][h * 16 : h * 16 + 16]], axis=0)
        w0[v] = jnp.where(lane < 16, side, jnp.where(lane < 72, pltpu.roll(own, 16, 1), own))

    first, nose = blk == 0, blk == BLK - 1
    even_row = iota((ROWS, LANES), 0) % 2 == 0

    def fix(ref):
        set_ghost_rows(ref, wn)

        @pl.when(first)
        def _():
            for v in range(14):
                w = ref[v]
                ref[v] = jnp.where(lane == 15, pltpu.roll(w, LANES - 1, 1), w)

        @pl.when(nose)
        def _():
            for v in range(14):
                w = ref[v]
                moved = pltpu.roll(w, 1, 1)
                swapped = jnp.where(even_row, pltpu.roll(moved, ROWS - 1, 0), pltpu.roll(moved, 1, 0))
                ref[v] = jnp.where(lane == 0, swapped, w)

    lane_own = iota((OWN, LANES), 1)
    copies = []

    def emit(v, f, r):
        if v == 0:

            @pl.when(place == 0)
            def _():
                for copy in mains:
                    copy.wait()

        for i, (out, staged, late, new) in enumerate(((final, finals, late_final, f), (last, lasts, late_last, r))):
            old = jnp.where(place == 0, staged[v], late[v])
            staged[v] = jnp.where(lane_own < 3, pltpu.roll(new, LANES - 16, 1), jnp.where(lane_own >= 125, new, old))
            copy = pltpu.make_async_copy(staged.at[v], out.at[v], out_sems.at[i, v])
            copy.start()
            copies.append(copy)

    sections(fix, w0, wa, wb, coeff, shear, thermal, emit)
    for copy in copies:
        copy.wait()


VMEM = pl.BlockSpec(memory_space=pltpu.VMEM)
HBM = pl.BlockSpec(memory_space=pltpu.HBM)
ANY = pl.BlockSpec(memory_space=pl.ANY)
SMEM = pl.BlockSpec(memory_space=pltpu.SMEM)
SCRATCH = [pltpu.VMEM((14, ROWS, LANES), jnp.float32)] * 3 + [pltpu.VMEM((2, ROWS, LANES), jnp.float32)]
PARAMS = pltpu.CompilerParams(vmem_limit_bytes=12 * 1024 * 1024)


def f32(*shape):
    return jax.ShapeDtypeStruct(shape, jnp.float32)


def call(kernel, outs, ins, scratch=()):
    return pl.pallas_call(
        kernel, out_shape=outs, in_specs=ins, out_specs=tuple(VMEM for _ in outs), scratch_shapes=scratch, compiler_params=PARAMS,
        cost_estimate=pl.CostEstimate(flops=1, bytes_accessed=1, transcendentals=0),
    )


def at(blk, wn):
    return blk * WN + wn


def send(x, pairs):
    return lax.ppermute(x, ("blk", "wn"), pairs)


def wrap_pairs(shift):
    return [
        (at(b, w), at(b + 1, w + shift))
        for b in range(RUN - 1, BLK - 1, RUN)
        for w in range(WN)
        if 0 <= w + shift < WN
    ]


def swap(pairs):
    return pairs + [(target, source) for source, target in pairs]


def rows_pairs(start, early):
    return swap([
        (at(b, w), at(b, w + 1)) for b in range(BLK) if (b % RUN < 2 if early else b % RUN > 1) for w in range(start, WN - 1, 2)
    ])


def columns_pairs(places):
    return [(at(b, w), at(b + 1, w)) for b in range(BLK - 1) if b % RUN in places for w in range(WN)]


FIRST = swap(columns_pairs((0,)))
FORWARD = columns_pairs(range(1, RUN - 1))
BACKWARD = [(target, source) for source, target in FORWARD]
RELAY = [(at(b, w), at(b - 1, w)) for b in range(RUN, BLK, RUN) for w in range(WN)]


def idle(*outs):
    return tuple(pl.pallas_call(idle_kernel, out_shape=outs, out_specs=tuple(HBM for _ in outs))())


def in_hbm(x):
    return pltpu.with_memory_space_constraint(x, pltpu.HBM)


def local(species, flow, heat, shear, thermal):
    strips = f32(18, LANES)
    rows = f32(14, 8, LANES)
    halo_shape = f32(14, 16, LANES)
    out = f32(14, OWN, LANES)
    place = lax.axis_index("blk") % RUN
    shear, thermal = in_hbm(shear), in_hbm(thermal)
    block, right, corner = call(
        load_kernel,
        (out, f32(4, 8, LANES), f32(3, 8, LANES)),
        [HBM] * 3,
        [pltpu.SemaphoreType.DMA((3,))],
    )(in_hbm(species.reshape(11, OWN, LANES)), in_hbm(flow.reshape(2, OWN, LANES)), in_hbm(heat.reshape(1, OWN, LANES)))
    wrap_down = send(corner, wrap_pairs(1))
    wrap = send(right, wrap_pairs(0))
    wrap_up = send(corner, wrap_pairs(-1))

    def exchange_rows(block, early):
        second = call(second_rows_kernel, (rows,), [VMEM])(block)[0]
        second = send(second, rows_pairs(1, early))
        first = call(first_rows_kernel, (f32(84, LANES),), [VMEM, ANY])(block, block if early else second)[0]
        first = send(first, rows_pairs(0, early))
        return first, second

    def early(block, shear, thermal):
        first, second = exchange_rows(block, True)
        halo, pair, lows, highs = call(early_columns_kernel, (halo_shape, strips, strips, strips), [VMEM] * 3)(first, second, block)
        pair = send(pair, FIRST)
        final, last = lax.cond(place == 0, main, no_main, block, halo, shear, thermal)
        return halo, pair, lows, highs, final, last

    def not_early(block, shear, thermal):
        return idle(halo_shape, strips, strips, strips, out, out)

    def main(block, halo, shear, thermal):
        return tuple(call(early_main_kernel, (out, out), [VMEM] * 2 + [SMEM] * 2, SCRATCH)(block, halo, shear, thermal))

    def no_main(block, halo, shear, thermal):
        return idle(out, out)

    def edges(block, lows, highs):
        first, second = exchange_rows(block, False)
        return tuple(call(late_columns_kernel, (halo_shape, strips, strips), [VMEM] * 3)(first, second, block))

    def known_edges(block, lows, highs):
        return (*idle(halo_shape), *call(keep_kernel, (strips, strips), [VMEM] * 2)(lows, highs))

    def late(block, lows, highs):
        return lax.cond(place > 1, edges, known_edges, block, lows, highs)

    def not_late(block, lows, highs):
        return idle(halo_shape, strips, strips)

    def neighbours(block, shear, thermal):
        early_halo, early_pair, lows, highs, main_final, main_last = lax.cond(place <= 1, early, not_early, block, shear, thermal)

        def rest(block, lows, highs):
            relay = send(lows, RELAY)
            return (*lax.cond(place > 0, late, not_late, block, lows, highs), relay)

        def no_rest(block, lows, highs):
            return idle(halo_shape, strips, strips, strips)

        halo, lows, highs, relay = lax.cond(
            at(lax.axis_index("blk"), lax.axis_index("wn")) < 2 * at(BLK, WN), rest, no_rest, block, lows, highs
        )
        return early_halo, halo, early_pair, lows, highs, relay, main_final, main_last

    def none(block, shear, thermal):
        return idle(halo_shape, halo_shape, strips, strips, strips, strips, out, out)

    early_halo, halo, early_pair, lows, highs, relay, early_final, early_last = lax.cond(
        at(lax.axis_index("blk"), lax.axis_index("wn")) < at(BLK, WN), neighbours, none, block, shear, thermal
    )
    left = send(highs, FORWARD)
    right = send(lows, BACKWARD)
    halo, late_final, late_last = call(
        late_main_kernel, (halo_shape, out, out), [VMEM] + [HBM] * 2 + [SMEM] * 2, SCRATCH + [pltpu.SemaphoreType.DMA]
    )(block, early_halo, halo, shear, thermal)
    final, last = pl.pallas_call(
        last_kernel,
        out_shape=(out, out),
        in_specs=[VMEM] * 9 + [SMEM] * 2 + [HBM] * 2 + [VMEM] * 2,
        out_specs=(HBM, HBM),
        scratch_shapes=SCRATCH
        + [pltpu.VMEM((14, OWN, LANES), jnp.float32)] * 2
        + [pltpu.SemaphoreType.DMA((2,)), pltpu.SemaphoreType.DMA((2, 14))],
        compiler_params=PARAMS,
        cost_estimate=pl.CostEstimate(flops=1, bytes_accessed=1, transcendentals=0),
    )(
        block, halo, early_pair, left, right, relay, wrap, wrap_up, wrap_down, shear, thermal,
        early_final, early_last, late_final, late_last,
    )
    return final.reshape(14, 16, 2, LANES), last.reshape(14, 16, 2, LANES)


def solution(mesh):
    return jax.shard_map(
        local,
        mesh=mesh,
        in_specs=(P(None, "wn", None, "blk"), P(None, "wn", None, "blk"), P("wn", None, "blk"), P(), P()),
        out_specs=(P(None, "wn", None, "blk"), P(None, "wn", None, "blk")),
        check_vma=False,
    )
```

```python
import jax
import jax.numpy as jnp
import numpy as np
from jax import lax
from jax.experimental import pallas as pl
from jax.experimental.pallas import tpu as pltpu
from jax.sharding import PartitionSpec as P

MASSES = [28.0, 32.0, 30.0, 14.0, 16.0, 28.0, 32.0, 30.0, 14.0, 16.0, 0.00055]
STEP = 0.16
WN = 8
BLK = 96
RUN = 12
OWN = 32
ROWS = 48
LANES = 128
CHUNK = 24


def iota(shape, dim):
    return lax.broadcasted_iota(jnp.int32, shape, dim)


def set_ghost_rows(state, wn):
    sub = iota((8, LANES), 0)
    low, high = wn == 0, wn == WN - 1
    for v in range(14):
        first = state[v, 0:8]
        last = state[v, 24:32]
        above = state[v, 32:40]
        below = state[v, 40:48]
        state[v, 32:40] = jnp.where(high & (sub < 2), pltpu.roll(last, 2, 0), above)
        cut = jnp.where(sub == 6, pltpu.roll(first, 3, 0), pltpu.roll(first, 5, 0))
        state[v, 40:48] = jnp.where(low & (sub >= 6), cut, below)


def coefficients(state, coeff, table):
    for c in range(ROWS // CHUNK):
        rows = pl.ds(c * CHUNK, CHUNK)
        x = [state[r, rows] for r in range(11)]
        logs = jnp.log(state[13, rows])
        visc = cond = None
        for s in range(11):
            k = 11 * s
            dv = table[k : k + 1] * x[0]
            dc = table[k + 121 : k + 122] * x[0]
            for r in range(1, 11):
                k = 11 * s + r
                dv = dv + table[k : k + 1] * x[r]
                dc = dc + table[k + 121 : k + 122] * x[r]
            tv = x[s] * np.float32(MASSES[s] / 28.0) / dv
            tc = x[s] / dc
            visc = tv if visc is None else visc + tv
            cond = tc if cond is None else cond + tc
        coeff[0, rows] = jnp.exp(0.7 * logs) * (0.5 * visc)
        coeff[1, rows] = jnp.exp(0.5 * logs) * (0.5 * cond)


def faces(coeff):
    out = []
    for k in (coeff[1], coeff[0]):
        out.append((k + pltpu.roll(k, ROWS - 2, 0), k + pltpu.roll(k, LANES - 1, 1)))
    return out


def residual(w, face):
    down, across = face
    f = down * (pltpu.roll(w, ROWS - 2, 0) - w)
    g = across * (pltpu.roll(w, LANES - 1, 1) - w)
    return (f - pltpu.roll(f, 2, 0)) + (g - pltpu.roll(g, 1, 1))


def sections(fix, w0, wa, wb, coeff, table, emit):
    fix(w0)
    coefficients(w0, coeff, table)
    face = faces(coeff)
    for v in range(14):
        w = w0[v]
        wa[v] = w + STEP * residual(w, face[v in (11, 12)])
    fix(wa)
    coefficients(wa, coeff, table)
    face = faces(coeff)
    for v in range(14):
        w = wa[v]
        wb[v] = 0.75 * w0[v] + 0.25 * (w + STEP * residual(w, face[v in (11, 12)]))
    fix(wb)
    coefficients(wb, coeff, table)
    face = faces(coeff)
    for v in range(14):
        w = wb[v]
        last = residual(w, face[v in (11, 12)])
        final = w0[v] * np.float32(1.0 / 3.0) + np.float32(2.0 / 3.0) * (w + STEP * last)
        emit(v, final[:OWN], last[:OWN])


def pack_columns(rows):
    missing = -rows.shape[0] % LANES
    if missing:
        rows = jnp.concatenate([rows, jnp.zeros((missing, LANES), jnp.float32)], axis=0)
    left, right = [], []
    for t in range(rows.shape[0] // LANES):
        turned = rows[t * LANES : (t + 1) * LANES].T
        left.append(turned[:8])
        right.append(turned[120:])
    return left, right


def load_kernel(species, flow, heat, shear, thermal, block, right, corner, corner_again, table, matrices, sems):
    copies = [
        pltpu.make_async_copy(source, block.at[pl.ds(low, count)], sems.at[i])
        for i, (source, low, count) in enumerate(((species, 0, 11), (flow, 11, 2), (heat, 13, 1)))
    ]
    small = [pltpu.make_async_copy(source, matrices.at[i], sems.at[3 + i]) for i, source in enumerate((shear, thermal))]
    for copy in copies + small:
        copy.start()
    for copy in small:
        copy.wait()
    for i in range(2):
        for s in range(11):
            for r in range(11):
                k = 121 * i + 11 * s + r
                table[k : k + 1] = jnp.full((1, LANES), matrices[i, s, r], jnp.float32)
    for copy in copies:
        copy.wait()
    _, rights = pack_columns(block[...].reshape(14 * OWN, LANES))
    for t in range(4):
        right[t] = rights[t]
    low, high = block[:, 0:8], block[:, 24:32]
    _, rights = pack_columns(jnp.concatenate([low, high], axis=1).reshape(14 * 16, LANES))
    for t in range(4):
        corner[t] = rights[t % 2]
    for t in range(3):
        corner_again[t] = rights[t % 2]


def rows_kernel(block, second, first):
    even = lax.axis_index("wn") % 2 == 0
    second[...] = jnp.where(even, block[:, 0:8], block[:, 24:32])
    for v in range(14):
        first[pl.ds(6 * v, 6)] = jnp.where(even, block[v, 26:32], block[v, 0:6])


def join_kernel(value, a, b, c, out):
    pass


def halo_of(first, second):
    even = lax.axis_index("wn") % 2 == 0
    zeros = jnp.zeros((2, LANES), jnp.float32)
    two = second[...]
    one = [first[pl.ds(6 * v, 6)] for v in range(14)]
    above = jnp.stack([jnp.concatenate([x, zeros], axis=0) for x in one])
    below = jnp.stack([jnp.concatenate([zeros, x], axis=0) for x in one])
    return jnp.concatenate([jnp.where(even, above, two), jnp.where(even, two, below)], axis=1)


def columns_of(block, halo):
    lefts, rights = pack_columns(block[...].reshape(14 * OWN, LANES))
    lefts_halo, rights_halo = pack_columns(halo.reshape(14 * 16, LANES))
    return lefts + lefts_halo, rights + rights_halo


def early_columns_kernel(first, second, block, halo, pair, lows, highs, offer):
    even = lax.axis_index("blk") % 2 == 0
    halo[...] = halo_of(first, second)
    lefts, rights = columns_of(block, halo[...])
    for t in range(6):
        three = pl.ds(3 * t, 3)
        pair[three] = jnp.where(even, rights[t][5:8], lefts[t][0:3])
        lows[three] = lefts[t][0:3]
        offer[three] = lefts[t][0:3]
        highs[three] = rights[t][5:8]
    offer[18:20] = jnp.zeros((2, LANES), jnp.float32)


def late_columns_kernel(first, second, block, halo, lows, highs):
    halo[...] = halo_of(first, second)
    lefts, rights = columns_of(block, halo[...])
    for t in range(6):
        three = pl.ds(3 * t, 3)
        highs[three] = rights[t][5:8]
        lows[three] = lefts[t][0:3]


def keep_kernel(early_lows, early_highs, lows, highs):
    lows[...] = early_lows[...]
    highs[...] = early_highs[...]


def gather_rows(block, halo, w0):
    for v in range(14):
        w0[v, 0:OWN] = block[v]
        w0[v, OWN:ROWS] = halo[v]


def main_sections(block, halo, table, final, last, w0, wa, wb, coeff):
    wn = lax.axis_index("wn")
    if halo is not None:
        gather_rows(block, halo, w0)

    def emit(v, f, r):
        final[v] = f
        last[v] = r

    sections(lambda ref: set_ghost_rows(ref, wn), w0, wa, wb, coeff, table, emit)


def early_main_kernel(block, halo, table, final, last, w0, wa, wb, coeff):
    main_sections(block, halo, table, final, last, w0, wa, wb, coeff)


def idle_kernel(*refs):
    pass


def late_main_kernel(block, early_halo, late_halo, table, halo, final, last, w0, wa, wb, coeff, sem):
    place = lax.axis_index("blk") % RUN
    for known, source in ((place <= 1, early_halo), (place > 1, late_halo)):

        @pl.when(known)
        def _():
            copy = pltpu.make_async_copy(source, halo, sem)
            copy.start()
            copy.wait()

    @pl.when(place != 0)
    def _():
        main_sections(block, halo, table, final, last, w0, wa, wb, coeff)


def last_kernel(
    block, halo, early_pair, left, right, relay, wrap, wrap_up, wrap_down, table,
    early_final, early_last, late_final, late_last, final, last, w0, wa, wb, coeff, finals, lasts, in_sems, out_sems,
):
    wn = lax.axis_index("wn")
    blk = lax.axis_index("blk")
    place = blk % RUN
    mains = [pltpu.make_async_copy(a, b, in_sems.at[i]) for i, (a, b) in enumerate(((early_final, finals), (early_last, lasts)))]

    @pl.when(place == 0)
    def _():
        for copy in mains:
            copy.start()

    lane = iota((ROWS, LANES), 1)
    gather_rows(block, halo, w0)
    lane3 = iota((3, LANES), 1)
    tiles = []
    for t in range(6):
        three = pl.ds(3 * t, 3)
        if t < 4:
            from_wrap = wrap[t, 5:8]
        else:
            from_wrap = jnp.where(lane3 % 16 < 8, wrap_up[t - 4, 5:8], wrap_down[t - 4, 5:8])
        lo = jnp.where(place == 0, from_wrap, jnp.where(place == 1, early_pair[three], left[three]))
        hi = jnp.where(place == RUN - 1, relay[three], jnp.where(place == 0, early_pair[three], right[three]))
        full = jnp.concatenate([hi, jnp.zeros((10, LANES), jnp.float32), lo, jnp.zeros((112, LANES), jnp.float32)], axis=0)
        tiles.append(full.T)
    for v in range(14):
        own = w0[v]
        q, h = v % 4, v % 8
        side = jnp.concatenate([tiles[v // 4][q * 32 : q * 32 + 32], tiles[4 + v // 8][h * 16 : h * 16 + 16]], axis=0)
        w0[v] = jnp.where(lane < 16, side, jnp.where(lane < 72, pltpu.roll(own, 16, 1), own))

    first, nose = blk == 0, blk == BLK - 1
    even_row = iota((ROWS, LANES), 0) % 2 == 0

    def fix(ref):
        set_ghost_rows(ref, wn)

        @pl.when(first)
        def _():
            for v in range(14):
                w = ref[v]
                ref[v] = jnp.where(lane == 15, pltpu.roll(w, LANES - 1, 1), w)

        @pl.when(nose)
        def _():
            for v in range(14):
                w = ref[v]
                moved = pltpu.roll(w, 1, 1)
                swapped = jnp.where(even_row, pltpu.roll(moved, ROWS - 1, 0), pltpu.roll(moved, 1, 0))
                ref[v] = jnp.where(lane == 0, swapped, w)

    lane_own = iota((OWN, LANES), 1)
    copies = []

    def emit(v, f, r):
        if v == 0:

            @pl.when(place == 0)
            def _():
                for copy in mains:
                    copy.wait()

        parts = ((final, finals, late_final, f), (last, lasts, late_last, r))
        for i, (out, staged, late, new) in enumerate(parts):
            old = jnp.where(place == 0, staged[v], late[v])
            staged[v] = jnp.where(lane_own < 3, pltpu.roll(new, LANES - 16, 1), jnp.where(lane_own >= 125, new, old))
            copy = pltpu.make_async_copy(staged.at[v], out.at[v], out_sems.at[i, v])
            copy.start()
            copies.append(copy)

    sections(fix, w0, wa, wb, coeff, table, emit)
    for copy in copies:
        copy.wait()


VMEM = pl.BlockSpec(memory_space=pltpu.VMEM)
HBM = pl.BlockSpec(memory_space=pltpu.HBM)
ANY = pl.BlockSpec(memory_space=pl.ANY)
SMEM = pl.BlockSpec(memory_space=pltpu.SMEM)
SCRATCH = [pltpu.VMEM((14, ROWS, LANES), jnp.float32)] * 3 + [pltpu.VMEM((2, ROWS, LANES), jnp.float32)]
PARAMS = pltpu.CompilerParams(vmem_limit_bytes=12 * 1024 * 1024)


def f32(*shape):
    return jax.ShapeDtypeStruct(shape, jnp.float32)


def call(kernel, outs, ins, scratch=()):
    return pl.pallas_call(
        kernel, out_shape=outs, in_specs=ins, out_specs=tuple(VMEM for _ in outs), scratch_shapes=scratch, compiler_params=PARAMS,
        cost_estimate=pl.CostEstimate(flops=1, bytes_accessed=1, transcendentals=0),
    )


def at(blk, wn):
    return blk * WN + wn


def send(x, pairs):
    return lax.ppermute(x, ("blk", "wn"), pairs)


def wrap_pairs(shift):
    return [
        (at(b, w), at(b + 1, w + shift))
        for b in range(RUN - 1, BLK - 1, RUN)
        for w in range(WN)
        if 0 <= w + shift < WN
    ]


def swap(pairs):
    return pairs + [(target, source) for source, target in pairs]


def rows_pairs(start, early):
    return swap([
        (at(b, w), at(b, w + 1)) for b in range(BLK) if (b % RUN < 2 if early else b % RUN > 1) for w in range(start, WN - 1, 2)
    ])


def columns_pairs(places):
    return [(at(b, w), at(b + 1, w)) for b in range(BLK - 1) if b % RUN in places for w in range(WN)]


FIRST = swap(columns_pairs((0,)))
FORWARD = columns_pairs(range(1, RUN - 1))
BACKWARD = [(target, source) for source, target in FORWARD]
RELAY = [(at(b, w), at(b - 1, w)) for b in range(RUN, BLK, RUN) for w in range(WN)]


def idle(*outs):
    return tuple(pl.pallas_call(idle_kernel, out_shape=outs, out_specs=tuple(HBM for _ in outs))())


def in_hbm(x):
    return pltpu.with_memory_space_constraint(x, pltpu.HBM)


def local(species, flow, heat, shear, thermal):
    strips = f32(18, LANES)
    offered = f32(20, LANES)
    rows = f32(14, 8, LANES)
    halo_shape = f32(14, 16, LANES)
    out = f32(14, OWN, LANES)
    place = lax.axis_index("blk") % RUN
    block, right, corner, corner_again, table = call(
        load_kernel,
        (out, f32(4, 8, LANES), f32(4, 8, LANES), f32(3, 8, LANES), f32(248, LANES)),
        [HBM] * 5,
        [pltpu.SMEM((2, 11, 11), jnp.float32), pltpu.SemaphoreType.DMA((5,))],
    )(
        in_hbm(species.reshape(11, OWN, LANES)),
        in_hbm(flow.reshape(2, OWN, LANES)),
        in_hbm(heat.reshape(1, OWN, LANES)),
        in_hbm(shear),
        in_hbm(thermal),
    )
    wrap_down = send(corner_again, wrap_pairs(1))
    wrap = send(right, wrap_pairs(0))
    wrap_up = send(corner, wrap_pairs(-1))

    def exchange_rows(block, early):
        second, first = call(rows_kernel, (rows, f32(84, LANES)), [VMEM])(block)
        return send(first, rows_pairs(0, early)), send(second, rows_pairs(1, early))

    def early(block, table):
        first, second = exchange_rows(block, True)
        halo, pair, lows, highs, offer = call(early_columns_kernel, (halo_shape, strips, strips, strips, offered), [VMEM] * 3)(
            first, second, block
        )
        pair = send(pair, FIRST)
        final, last = lax.cond(place == 0, main, no_main, block, halo, table)
        return halo, pair, lows, highs, offer, final, last

    def not_early(block, table):
        return idle(halo_shape, strips, strips, strips, offered, out, out)

    def main(block, halo, table):
        return tuple(call(early_main_kernel, (out, out), [VMEM] * 3, SCRATCH)(block, halo, table))

    def no_main(block, halo, table):
        return idle(out, out)

    def edges(block, lows, highs):
        first, second = exchange_rows(block, False)
        return tuple(call(late_columns_kernel, (halo_shape, strips, strips), [VMEM] * 3)(first, second, block))

    def known_edges(block, lows, highs):
        return (*idle(halo_shape), *call(keep_kernel, (strips, strips), [VMEM] * 2)(lows, highs))

    def late(block, lows, highs):
        return lax.cond(place > 1, edges, known_edges, block, lows, highs)

    def not_late(block, lows, highs):
        return idle(halo_shape, strips, strips)

    early_halo, early_pair, lows, highs, offer, early_final, early_last = lax.cond(place <= 1, early, not_early, block, table)
    relay = send(offer, RELAY)
    lows = pl.pallas_call(
        join_kernel,
        out_shape=strips,
        in_specs=[ANY] * 4,
        out_specs=ANY,
        input_output_aliases={0: 0},
        cost_estimate=pl.CostEstimate(flops=1, bytes_accessed=1, transcendentals=0),
    )(lows, wrap, wrap_up, wrap_down)
    halo, lows, highs = lax.cond(place > 0, late, not_late, block, lows, highs)
    left = send(highs, FORWARD)
    right = send(lows, BACKWARD)
    halo, late_final, late_last = call(
        late_main_kernel, (halo_shape, out, out), [VMEM, HBM, HBM, VMEM], SCRATCH + [pltpu.SemaphoreType.DMA]
    )(block, in_hbm(early_halo), in_hbm(halo), table)
    final, last = pl.pallas_call(
        last_kernel,
        out_shape=(out, out),
        in_specs=[VMEM] * 10 + [HBM] * 2 + [VMEM] * 2,
        out_specs=(HBM, HBM),
        scratch_shapes=SCRATCH
        + [pltpu.VMEM((14, OWN, LANES), jnp.float32)] * 2
        + [pltpu.SemaphoreType.DMA((2,)), pltpu.SemaphoreType.DMA((2, 14))],
        compiler_params=PARAMS,
        cost_estimate=pl.CostEstimate(flops=1, bytes_accessed=1, transcendentals=0),
    )(
        block, halo, early_pair, left, right, relay, wrap, wrap_up, wrap_down, table,
        in_hbm(early_final), in_hbm(early_last), late_final, late_last,
    )
    return final.reshape(14, 16, 2, LANES), last.reshape(14, 16, 2, LANES)


def solution(mesh):
    return jax.shard_map(
        local,
        mesh=mesh,
        in_specs=(P(None, "wn", None, "blk"), P(None, "wn", None, "blk"), P("wn", None, "blk"), P(), P()),
        out_specs=(P(None, "wn", None, "blk"), P(None, "wn", None, "blk")),
        check_vma=False,
    )
```

```python
import jax
import jax.numpy as jnp
import numpy as np
from jax import lax
from jax.experimental import pallas as pl
from jax.experimental.pallas import tpu as pltpu
from jax.sharding import PartitionSpec as P

MASSES = [28.0, 32.0, 30.0, 14.0, 16.0, 28.0, 32.0, 30.0, 14.0, 16.0, 0.00055]
STEP = 0.16
WN = 8
BLK = 96
RUN = 12
OWN = 32
ROWS = 48
LANES = 128
CHUNK = 24


def iota(shape, dim):
    return lax.broadcasted_iota(jnp.int32, shape, dim)


def set_ghost_rows(state, wn):
    sub = iota((8, LANES), 0)
    low, high = wn == 0, wn == WN - 1
    for v in range(14):
        first = state[v, 0:8]
        last = state[v, 24:32]
        above = state[v, 32:40]
        below = state[v, 40:48]
        state[v, 32:40] = jnp.where(high & (sub < 2), pltpu.roll(last, 2, 0), above)
        cut = jnp.where(sub == 6, pltpu.roll(first, 3, 0), pltpu.roll(first, 5, 0))
        state[v, 40:48] = jnp.where(low & (sub >= 6), cut, below)


def coefficients(state, coeff, table):
    for c in range(ROWS // CHUNK):
        rows = pl.ds(c * CHUNK, CHUNK)
        x = [state[r, rows] for r in range(11)]
        logs = jnp.log(state[13, rows])
        visc = cond = None
        for s in range(11):
            k = 11 * s
            dv = table[k : k + 1] * x[0]
            dc = table[k + 121 : k + 122] * x[0]
            for r in range(1, 11):
                k = 11 * s + r
                dv = dv + table[k : k + 1] * x[r]
                dc = dc + table[k + 121 : k + 122] * x[r]
            tv = x[s] * np.float32(MASSES[s] / 28.0) / dv
            tc = x[s] / dc
            visc = tv if visc is None else visc + tv
            cond = tc if cond is None else cond + tc
        coeff[0, rows] = jnp.exp(0.7 * logs) * (0.5 * visc)
        coeff[1, rows] = jnp.exp(0.5 * logs) * (0.5 * cond)


def faces(coeff):
    for index, fields in ((1, (*range(11), 13)), (0, (11, 12))):
        k = coeff[index]
        face = (k + pltpu.roll(k, ROWS - 2, 0), k + pltpu.roll(k, LANES - 1, 1))
        for v in fields:
            yield v, face


def residual(w, face):
    down, across = face
    f = down * (pltpu.roll(w, ROWS - 2, 0) - w)
    g = across * (pltpu.roll(w, LANES - 1, 1) - w)
    return (f - pltpu.roll(f, 2, 0)) + (g - pltpu.roll(g, 1, 1))


def sections(fix, w0, wa, wb, coeff, table, emit):
    fix(w0)
    coefficients(w0, coeff, table)
    for v, face in faces(coeff):
        w = w0[v]
        wa[v] = w + STEP * residual(w, face)
    fix(wa)
    coefficients(wa, coeff, table)
    for v, face in faces(coeff):
        w = wa[v]
        wb[v] = 0.75 * w0[v] + 0.25 * (w + STEP * residual(w, face))
    fix(wb)
    coefficients(wb, coeff, table)
    for v, face in faces(coeff):
        w = wb[v]
        last = residual(w, face)
        final = w0[v] * np.float32(1.0 / 3.0) + np.float32(2.0 / 3.0) * (w + STEP * last)
        emit(v, final[:OWN], last[:OWN])


def pack_columns(rows):
    missing = -rows.shape[0] % LANES
    if missing:
        rows = jnp.concatenate([rows, jnp.zeros((missing, LANES), jnp.float32)], axis=0)
    left, right = [], []
    for t in range(rows.shape[0] // LANES):
        turned = rows[t * LANES : (t + 1) * LANES].T
        left.append(turned[:8])
        right.append(turned[120:])
    return left, right


def load_kernel(species, flow, heat, shear, thermal, block, right, corner, corner_again, table, matrices, sems):
    copies = [
        pltpu.make_async_copy(source, block.at[pl.ds(low, count)], sems.at[i])
        for i, (source, low, count) in enumerate(((species, 0, 11), (flow, 11, 2), (heat, 13, 1)))
    ]
    small = [pltpu.make_async_copy(source, matrices.at[i], sems.at[3 + i]) for i, source in enumerate((shear, thermal))]
    for copy in copies + small:
        copy.start()
    for copy in small:
        copy.wait()
    for i in range(2):
        for s in range(11):
            for r in range(11):
                k = 121 * i + 11 * s + r
                table[k : k + 1] = jnp.full((1, LANES), matrices[i, s, r], jnp.float32)
    for copy in copies:
        copy.wait()
    _, rights = pack_columns(block[...].reshape(14 * OWN, LANES))
    for t in range(4):
        right[t] = rights[t]
    low, high = block[:, 0:8], block[:, 24:32]
    _, rights = pack_columns(jnp.concatenate([low, high], axis=1).reshape(14 * 16, LANES))
    for t in range(4):
        corner[t] = rights[t % 2]
    for t in range(3):
        corner_again[t] = rights[t % 2]


def rows_kernel(block, second, first):
    even = lax.axis_index("wn") % 2 == 0
    second[...] = jnp.where(even, block[:, 0:8], block[:, 24:32])
    for v in range(14):
        first[pl.ds(6 * v, 6)] = jnp.where(even, block[v, 26:32], block[v, 0:6])


def join_kernel(value, a, b, c, out):
    pass


def halo_of(first, second):
    even = lax.axis_index("wn") % 2 == 0
    zeros = jnp.zeros((2, LANES), jnp.float32)
    two = second[...]
    one = [first[pl.ds(6 * v, 6)] for v in range(14)]
    above = jnp.stack([jnp.concatenate([x, zeros], axis=0) for x in one])
    below = jnp.stack([jnp.concatenate([zeros, x], axis=0) for x in one])
    return jnp.concatenate([jnp.where(even, above, two), jnp.where(even, two, below)], axis=1)


def columns_of(block, halo):
    lefts, rights = pack_columns(block[...].reshape(14 * OWN, LANES))
    lefts_halo, rights_halo = pack_columns(halo.reshape(14 * 16, LANES))
    return lefts + lefts_halo, rights + rights_halo


def early_columns_kernel(first, second, block, halo, pair, lows, highs, offer):
    even = lax.axis_index("blk") % 2 == 0
    halo[...] = halo_of(first, second)
    lefts, rights = columns_of(block, halo[...])
    for t in range(6):
        three = pl.ds(3 * t, 3)
        pair[three] = jnp.where(even, rights[t][5:8], lefts[t][0:3])
        lows[three] = lefts[t][0:3]
        offer[three] = lefts[t][0:3]
        highs[three] = rights[t][5:8]
    offer[18:20] = jnp.zeros((2, LANES), jnp.float32)


def late_columns_kernel(first, second, block, halo, lows, highs):
    halo[...] = halo_of(first, second)
    lefts, rights = columns_of(block, halo[...])
    for t in range(6):
        three = pl.ds(3 * t, 3)
        highs[three] = rights[t][5:8]
        lows[three] = lefts[t][0:3]


def keep_kernel(early_lows, early_highs, lows, highs):
    lows[...] = early_lows[...]
    highs[...] = early_highs[...]


def gather_rows(block, halo, w0):
    for v in range(14):
        w0[v, 0:OWN] = block[v]
        w0[v, OWN:ROWS] = halo[v]


def main_sections(block, halo, table, final, last, w0, wa, wb, coeff):
    wn = lax.axis_index("wn")
    if halo is not None:
        gather_rows(block, halo, w0)

    def emit(v, f, r):
        final[v] = f
        last[v] = r

    sections(lambda ref: set_ghost_rows(ref, wn), w0, wa, wb, coeff, table, emit)


def early_main_kernel(block, halo, table, final, last, w0, wa, wb, coeff):
    main_sections(block, halo, table, final, last, w0, wa, wb, coeff)


def idle_kernel(*refs):
    pass


def late_main_kernel(block, early_halo, late_halo, table, halo, final, last, w0, wa, wb, coeff, sem):
    place = lax.axis_index("blk") % RUN
    for known, source in ((place <= 1, early_halo), (place > 1, late_halo)):

        @pl.when(known)
        def _():
            copy = pltpu.make_async_copy(source, halo, sem)
            copy.start()
            copy.wait()

    @pl.when(place != 0)
    def _():
        main_sections(block, halo, table, final, last, w0, wa, wb, coeff)


def last_kernel(
    block, halo, early_pair, left, right, relay, wrap, wrap_up, wrap_down, table,
    early_final, early_last, late_final, late_last, final, last, w0, wa, wb, coeff, finals, lasts, pair_rows, in_sems, out_sems,
):
    wn = lax.axis_index("wn")
    blk = lax.axis_index("blk")
    place = blk % RUN
    mains = [pltpu.make_async_copy(a, b, in_sems.at[i]) for i, (a, b) in enumerate(((early_final, finals), (early_last, lasts)))]

    beside = pltpu.make_async_copy(early_pair, pair_rows, in_sems.at[2])

    @pl.when(place <= 1)
    def _():
        beside.start()

    @pl.when(place == 0)
    def _():
        for copy in mains:
            copy.start()

    lane = iota((ROWS, LANES), 1)
    gather_rows(block, halo, w0)

    @pl.when(place <= 1)
    def _():
        beside.wait()

    lane3 = iota((3, LANES), 1)
    tiles = []
    for t in range(6):
        three = pl.ds(3 * t, 3)
        if t < 4:
            from_wrap = wrap[t, 5:8]
        else:
            from_wrap = jnp.where(lane3 % 16 < 8, wrap_up[t - 4, 5:8], wrap_down[t - 4, 5:8])
        lo = jnp.where(place == 0, from_wrap, jnp.where(place == 1, pair_rows[three], left[three]))
        hi = jnp.where(place == RUN - 1, relay[three], jnp.where(place == 0, pair_rows[three], right[three]))
        full = jnp.concatenate([hi, jnp.zeros((10, LANES), jnp.float32), lo, jnp.zeros((112, LANES), jnp.float32)], axis=0)
        tiles.append(full.T)
    for v in range(14):
        own = w0[v]
        q, h = v % 4, v % 8
        side = jnp.concatenate([tiles[v // 4][q * 32 : q * 32 + 32], tiles[4 + v // 8][h * 16 : h * 16 + 16]], axis=0)
        w0[v] = jnp.where(lane < 16, side, jnp.where(lane < 72, pltpu.roll(own, 16, 1), own))

    first, nose = blk == 0, blk == BLK - 1
    even_row = iota((ROWS, LANES), 0) % 2 == 0

    def fix(ref):
        set_ghost_rows(ref, wn)

        @pl.when(first)
        def _():
            for v in range(14):
                w = ref[v]
                ref[v] = jnp.where(lane == 15, pltpu.roll(w, LANES - 1, 1), w)

        @pl.when(nose)
        def _():
            for v in range(14):
                w = ref[v]
                moved = pltpu.roll(w, 1, 1)
                swapped = jnp.where(even_row, pltpu.roll(moved, ROWS - 1, 0), pltpu.roll(moved, 1, 0))
                ref[v] = jnp.where(lane == 0, swapped, w)

    lane_own = iota((OWN, LANES), 1)
    copies = []

    def emit(v, f, r):
        if v == 0:

            @pl.when(place == 0)
            def _():
                for copy in mains:
                    copy.wait()

        parts = ((final, finals, late_final, f), (last, lasts, late_last, r))
        for i, (out, staged, late, new) in enumerate(parts):
            old = jnp.where(place == 0, staged[v], late[v])
            staged[v] = jnp.where(lane_own < 3, pltpu.roll(new, LANES - 16, 1), jnp.where(lane_own >= 125, new, old))
            copy = pltpu.make_async_copy(staged.at[v], out.at[v], out_sems.at[i, v])
            copy.start()
            copies.append(copy)

    sections(fix, w0, wa, wb, coeff, table, emit)
    for copy in copies:
        copy.wait()


VMEM = pl.BlockSpec(memory_space=pltpu.VMEM)
HBM = pl.BlockSpec(memory_space=pltpu.HBM)
ANY = pl.BlockSpec(memory_space=pl.ANY)
SMEM = pl.BlockSpec(memory_space=pltpu.SMEM)
SCRATCH = [pltpu.VMEM((14, ROWS, LANES), jnp.float32)] * 3 + [pltpu.VMEM((2, ROWS, LANES), jnp.float32)]
PARAMS = pltpu.CompilerParams(vmem_limit_bytes=12 * 1024 * 1024)


def f32(*shape):
    return jax.ShapeDtypeStruct(shape, jnp.float32)


def call(kernel, outs, ins, scratch=()):
    return pl.pallas_call(
        kernel, out_shape=outs, in_specs=ins, out_specs=tuple(VMEM for _ in outs), scratch_shapes=scratch, compiler_params=PARAMS,
        cost_estimate=pl.CostEstimate(flops=1, bytes_accessed=1, transcendentals=0),
    )


def at(blk, wn):
    return blk * WN + wn


def send(x, pairs):
    return lax.ppermute(x, ("blk", "wn"), pairs)


def wrap_pairs(shift):
    return [
        (at(b, w), at(b + 1, w + shift))
        for b in range(RUN - 1, BLK - 1, RUN)
        for w in range(WN)
        if 0 <= w + shift < WN
    ]


def swap(pairs):
    return pairs + [(target, source) for source, target in pairs]


def rows_pairs(start, early):
    return swap([
        (at(b, w), at(b, w + 1)) for b in range(BLK) if (b % RUN < 2 if early else b % RUN > 1) for w in range(start, WN - 1, 2)
    ])


def columns_pairs(places):
    return [(at(b, w), at(b + 1, w)) for b in range(BLK - 1) if b % RUN in places for w in range(WN)]


FIRST = swap(columns_pairs((0,)))
FORWARD = columns_pairs(range(1, RUN - 1))
BACKWARD = [(target, source) for source, target in FORWARD]
RELAY = [(at(b, w), at(b - 1, w)) for b in range(RUN, BLK, RUN) for w in range(WN)]


def idle(*outs):
    return tuple(pl.pallas_call(idle_kernel, out_shape=outs, out_specs=tuple(HBM for _ in outs))())


def in_hbm(x):
    return pltpu.with_memory_space_constraint(x, pltpu.HBM)


def local(species, flow, heat, shear, thermal):
    strips = f32(18, LANES)
    offered = f32(20, LANES)
    rows = f32(14, 8, LANES)
    halo_shape = f32(14, 16, LANES)
    out = f32(14, OWN, LANES)
    place = lax.axis_index("blk") % RUN
    block, right, corner, corner_again, table = call(
        load_kernel,
        (out, f32(4, 8, LANES), f32(4, 8, LANES), f32(3, 8, LANES), f32(248, LANES)),
        [HBM] * 5,
        [pltpu.SMEM((2, 11, 11), jnp.float32), pltpu.SemaphoreType.DMA((5,))],
    )(
        in_hbm(species.reshape(11, OWN, LANES)),
        in_hbm(flow.reshape(2, OWN, LANES)),
        in_hbm(heat.reshape(1, OWN, LANES)),
        in_hbm(shear),
        in_hbm(thermal),
    )
    wrap_down = send(corner_again, wrap_pairs(1))
    wrap = send(right, wrap_pairs(0))
    wrap_up = send(corner, wrap_pairs(-1))

    def exchange_rows(block, early):
        second, first = call(rows_kernel, (rows, f32(84, LANES)), [VMEM])(block)
        return send(first, rows_pairs(0, early)), send(second, rows_pairs(1, early))

    def early(block, table):
        first, second = exchange_rows(block, True)
        halo, pair, lows, highs, offer = call(early_columns_kernel, (halo_shape, strips, strips, strips, offered), [VMEM] * 3)(
            first, second, block
        )
        pair = send(pair, FIRST)
        final, last = lax.cond(place == 0, main, no_main, block, halo, table)
        return halo, pair, lows, highs, offer, final, last

    def not_early(block, table):
        return idle(halo_shape, strips, strips, strips, offered, out, out)

    def main(block, halo, table):
        return tuple(call(early_main_kernel, (out, out), [VMEM] * 3, SCRATCH)(block, halo, table))

    def no_main(block, halo, table):
        return idle(out, out)

    def edges(block, lows, highs):
        first, second = exchange_rows(block, False)
        return tuple(call(late_columns_kernel, (halo_shape, strips, strips), [VMEM] * 3)(first, second, block))

    def known_edges(block, lows, highs):
        return (*idle(halo_shape), *call(keep_kernel, (strips, strips), [VMEM] * 2)(lows, highs))

    def late(block, lows, highs):
        return lax.cond(place > 1, edges, known_edges, block, lows, highs)

    def not_late(block, lows, highs):
        return idle(halo_shape, strips, strips)

    early_halo, early_pair, lows, highs, offer, early_final, early_last = lax.cond(place <= 1, early, not_early, block, table)
    relay = send(offer, RELAY)
    lows = pl.pallas_call(
        join_kernel,
        out_shape=strips,
        in_specs=[ANY] * 4,
        out_specs=ANY,
        input_output_aliases={0: 0},
        cost_estimate=pl.CostEstimate(flops=1, bytes_accessed=1, transcendentals=0),
    )(lows, wrap, wrap_up, wrap_down)
    halo, lows, highs = lax.cond(place > 0, late, not_late, block, lows, highs)
    left = send(highs, FORWARD)
    right = send(lows, BACKWARD)
    halo, late_final, late_last = call(
        late_main_kernel, (halo_shape, out, out), [VMEM, HBM, HBM, VMEM], SCRATCH + [pltpu.SemaphoreType.DMA]
    )(block, in_hbm(early_halo), in_hbm(halo), table)
    final, last = pl.pallas_call(
        last_kernel,
        out_shape=(out, out),
        in_specs=[VMEM] * 2 + [HBM] + [VMEM] * 7 + [HBM] * 2 + [VMEM] * 2,
        out_specs=(HBM, HBM),
        scratch_shapes=SCRATCH
        + [pltpu.VMEM((14, OWN, LANES), jnp.float32)] * 2
        + [pltpu.VMEM((18, LANES), jnp.float32), pltpu.SemaphoreType.DMA((3,)), pltpu.SemaphoreType.DMA((2, 14))],
        compiler_params=PARAMS,
        cost_estimate=pl.CostEstimate(flops=1, bytes_accessed=1, transcendentals=0),
    )(
        block, halo, in_hbm(early_pair), left, right, relay, wrap, wrap_up, wrap_down, table,
        in_hbm(early_final), in_hbm(early_last), late_final, late_last,
    )
    return final.reshape(14, 16, 2, LANES), last.reshape(14, 16, 2, LANES)


def solution(mesh):
    return jax.shard_map(
        local,
        mesh=mesh,
        in_specs=(P(None, "wn", None, "blk"), P(None, "wn", None, "blk"), P("wn", None, "blk"), P(), P()),
        out_specs=(P(None, "wn", None, "blk"), P(None, "wn", None, "blk")),
        check_vma=False,
    )
```

```python
import jax
import jax.numpy as jnp
import numpy as np
from jax import lax
from jax.experimental import pallas as pl
from jax.experimental.pallas import tpu as pltpu
from jax.sharding import PartitionSpec as P

MASSES = [28.0, 32.0, 30.0, 14.0, 16.0, 28.0, 32.0, 30.0, 14.0, 16.0, 0.00055]
STEP = 0.16
WN = 8
BLK = 96
RUN = 12
OWN = 32
ROWS = 48
LANES = 128
CHUNK = 24


def iota(shape, dim):
    return lax.broadcasted_iota(jnp.int32, shape, dim)


def set_ghost_rows(state, wn):
    sub = iota((8, LANES), 0)
    low, high = wn == 0, wn == WN - 1
    for v in range(14):
        first = state[v, 0:8]
        last = state[v, 24:32]
        above = state[v, 32:40]
        below = state[v, 40:48]
        state[v, 32:40] = jnp.where(high & (sub < 2), pltpu.roll(last, 2, 0), above)
        cut = jnp.where(sub == 6, pltpu.roll(first, 3, 0), pltpu.roll(first, 5, 0))
        state[v, 40:48] = jnp.where(low & (sub >= 6), cut, below)


def coefficients(state, coeff, table):
    for c in range(ROWS // CHUNK):
        rows = pl.ds(c * CHUNK, CHUNK)
        x = [state[r, rows] for r in range(11)]
        logs = jnp.log(state[13, rows])
        visc = cond = None
        for s in range(11):
            k = 11 * s
            dv = table[k : k + 1] * x[0]
            dc = table[k + 121 : k + 122] * x[0]
            for r in range(1, 11):
                k = 11 * s + r
                dv = dv + table[k : k + 1] * x[r]
                dc = dc + table[k + 121 : k + 122] * x[r]
            tv = x[s] * np.float32(MASSES[s] / 28.0) / dv
            tc = x[s] / dc
            visc = tv if visc is None else visc + tv
            cond = tc if cond is None else cond + tc
        coeff[0, rows] = jnp.exp(0.7 * logs) * (0.5 * visc)
        coeff[1, rows] = jnp.exp(0.5 * logs) * (0.5 * cond)


def faces(coeff):
    for index, fields in ((1, (*range(11), 13)), (0, (11, 12))):
        k = coeff[index]
        face = (k + pltpu.roll(k, ROWS - 2, 0), k + pltpu.roll(k, LANES - 1, 1))
        for v in fields:
            yield v, face


def residual(w, face):
    down, across = face
    f = down * (pltpu.roll(w, ROWS - 2, 0) - w)
    g = across * (pltpu.roll(w, LANES - 1, 1) - w)
    return (f - pltpu.roll(f, 2, 0)) + (g - pltpu.roll(g, 1, 1))


def sections(fix, w0, wa, wb, coeff, table, emit):
    fix(w0)
    coefficients(w0, coeff, table)
    for v, face in faces(coeff):
        w = w0[v]
        wa[v] = w + STEP * residual(w, face)
    fix(wa)
    coefficients(wa, coeff, table)
    for v, face in faces(coeff):
        w = wa[v]
        wb[v] = 0.75 * w0[v] + 0.25 * (w + STEP * residual(w, face))
    fix(wb)
    coefficients(wb, coeff, table)
    for v, face in faces(coeff):
        w = wb[v]
        last = residual(w, face)
        final = w0[v] * np.float32(1.0 / 3.0) + np.float32(2.0 / 3.0) * (w + STEP * last)
        emit(v, final[:OWN], last[:OWN])


def pack_columns(rows):
    missing = -rows.shape[0] % LANES
    if missing:
        rows = jnp.concatenate([rows, jnp.zeros((missing, LANES), jnp.float32)], axis=0)
    left, right = [], []
    for t in range(rows.shape[0] // LANES):
        turned = rows[t * LANES : (t + 1) * LANES].T
        left.append(turned[:8])
        right.append(turned[120:])
    return left, right


def load_kernel(species, flow, heat, shear, thermal, block, right, corner, corner_again, table, matrices, sems):
    copies = [
        pltpu.make_async_copy(source, block.at[pl.ds(low, count)], sems.at[i])
        for i, (source, low, count) in enumerate(((species, 0, 11), (flow, 11, 2), (heat, 13, 1)))
    ]
    small = [pltpu.make_async_copy(source, matrices.at[i], sems.at[3 + i]) for i, source in enumerate((shear, thermal))]
    for copy in copies + small:
        copy.start()
    for copy in small:
        copy.wait()
    for i in range(2):
        for s in range(11):
            for r in range(11):
                k = 121 * i + 11 * s + r
                table[k : k + 1] = jnp.full((1, LANES), matrices[i, s, r], jnp.float32)
    for copy in copies:
        copy.wait()
    _, rights = pack_columns(block[...].reshape(14 * OWN, LANES))
    for t in range(4):
        right[t] = rights[t]
    low, high = block[:, 0:8], block[:, 24:32]
    _, rights = pack_columns(jnp.concatenate([low, high], axis=1).reshape(14 * 16, LANES))
    for t in range(4):
        corner[t] = rights[t % 2]
    for t in range(3):
        corner_again[t] = rights[t % 2]


def rows_kernel(block, second, first):
    even = lax.axis_index("wn") % 2 == 0
    second[...] = jnp.where(even, block[:, 0:8], block[:, 24:32])
    for v in range(14):
        first[pl.ds(6 * v, 6)] = jnp.where(even, block[v, 26:32], block[v, 0:6])


def join_kernel(value, a, b, c, out):
    pass


def halo_of(first, second):
    even = lax.axis_index("wn") % 2 == 0
    zeros = jnp.zeros((2, LANES), jnp.float32)
    two = second[...]
    one = [first[pl.ds(6 * v, 6)] for v in range(14)]
    above = jnp.stack([jnp.concatenate([x, zeros], axis=0) for x in one])
    below = jnp.stack([jnp.concatenate([zeros, x], axis=0) for x in one])
    return jnp.concatenate([jnp.where(even, above, two), jnp.where(even, two, below)], axis=1)


def columns_of(block, halo):
    lefts, rights = pack_columns(block[...].reshape(14 * OWN, LANES))
    lefts_halo, rights_halo = pack_columns(halo.reshape(14 * 16, LANES))
    return lefts + lefts_halo, rights + rights_halo


def early_columns_kernel(first, second, block, halo, pair, lows, highs, offer):
    even = lax.axis_index("blk") % 2 == 0
    halo[...] = halo_of(first, second)
    lefts, rights = columns_of(block, halo[...])
    for t in range(6):
        three = pl.ds(3 * t, 3)
        pair[three] = jnp.where(even, rights[t][5:8], lefts[t][0:3])
        lows[three] = lefts[t][0:3]
        offer[three] = lefts[t][0:3]
        highs[three] = rights[t][5:8]
    offer[18:20] = jnp.zeros((2, LANES), jnp.float32)


def late_columns_kernel(first, second, block, halo, lows, highs):
    halo[...] = halo_of(first, second)
    lefts, rights = columns_of(block, halo[...])
    for t in range(6):
        three = pl.ds(3 * t, 3)
        highs[three] = rights[t][5:8]
        lows[three] = lefts[t][0:3]


def keep_kernel(early_lows, early_highs, lows, highs):
    lows[...] = early_lows[...]
    highs[...] = early_highs[...]


def gather_rows(block, halo, w0):
    for v in range(14):
        w0[v, 0:OWN] = block[v]
        w0[v, OWN:ROWS] = halo[v]


def main_sections(block, halo, table, final, last, w0, wa, wb, coeff):
    wn = lax.axis_index("wn")
    if halo is not None:
        gather_rows(block, halo, w0)

    def emit(v, f, r):
        final[v] = f
        last[v] = r

    sections(lambda ref: set_ghost_rows(ref, wn), w0, wa, wb, coeff, table, emit)


def early_main_kernel(block, halo, table, final, last, w0, wa, wb, coeff):
    main_sections(block, halo, table, final, last, w0, wa, wb, coeff)


def idle_kernel(*refs):
    pass


def late_main_kernel(block, early_halo, late_halo, early_pair, table, halo, pair, final, last, w0, wa, wb, coeff, sems):
    place = lax.axis_index("blk") % RUN

    @pl.when(place <= 1)
    def _():
        copies = [pltpu.make_async_copy(early_halo, halo, sems.at[0]), pltpu.make_async_copy(early_pair, pair, sems.at[1])]
        for copy in copies:
            copy.start()
        for copy in copies:
            copy.wait()

    @pl.when(place > 1)
    def _():
        copy = pltpu.make_async_copy(late_halo, halo, sems.at[0])
        copy.start()
        copy.wait()

    @pl.when(place != 0)
    def _():
        main_sections(block, halo, table, final, last, w0, wa, wb, coeff)


def last_kernel(
    block, halo, pair, left, right, relay, wrap, wrap_up, wrap_down, table,
    early_final, early_last, late_final, late_last, final, last, w0, wa, wb, coeff, finals, lasts, in_sems, out_sems,
):
    wn = lax.axis_index("wn")
    blk = lax.axis_index("blk")
    place = blk % RUN
    mains = [pltpu.make_async_copy(a, b, in_sems.at[i]) for i, (a, b) in enumerate(((early_final, finals), (early_last, lasts)))]

    @pl.when(place == 0)
    def _():
        for copy in mains:
            copy.start()

    lane = iota((ROWS, LANES), 1)
    gather_rows(block, halo, w0)

    lane3 = iota((3, LANES), 1)
    tiles = []
    for t in range(6):
        three = pl.ds(3 * t, 3)
        if t < 4:
            from_wrap = wrap[t, 5:8]
        else:
            from_wrap = jnp.where(lane3 % 16 < 8, wrap_up[t - 4, 5:8], wrap_down[t - 4, 5:8])
        lo = jnp.where(place == 0, from_wrap, jnp.where(place == 1, pair[three], left[three]))
        hi = jnp.where(place == RUN - 1, relay[three], jnp.where(place == 0, pair[three], right[three]))
        full = jnp.concatenate([hi, jnp.zeros((10, LANES), jnp.float32), lo, jnp.zeros((112, LANES), jnp.float32)], axis=0)
        tiles.append(full.T)
    for v in range(14):
        own = w0[v]
        q, h = v % 4, v % 8
        side = jnp.concatenate([tiles[v // 4][q * 32 : q * 32 + 32], tiles[4 + v // 8][h * 16 : h * 16 + 16]], axis=0)
        w0[v] = jnp.where(lane < 16, side, jnp.where(lane < 72, pltpu.roll(own, 16, 1), own))

    first, nose = blk == 0, blk == BLK - 1
    even_row = iota((ROWS, LANES), 0) % 2 == 0

    def fix(ref):
        set_ghost_rows(ref, wn)

        @pl.when(first)
        def _():
            for v in range(14):
                w = ref[v]
                ref[v] = jnp.where(lane == 15, pltpu.roll(w, LANES - 1, 1), w)

        @pl.when(nose)
        def _():
            for v in range(14):
                w = ref[v]
                moved = pltpu.roll(w, 1, 1)
                swapped = jnp.where(even_row, pltpu.roll(moved, ROWS - 1, 0), pltpu.roll(moved, 1, 0))
                ref[v] = jnp.where(lane == 0, swapped, w)

    lane_own = iota((OWN, LANES), 1)
    copies = []

    def emit(v, f, r):
        if v == 0:

            @pl.when(place == 0)
            def _():
                for copy in mains:
                    copy.wait()

        parts = ((final, finals, late_final, f), (last, lasts, late_last, r))
        for i, (out, staged, late, new) in enumerate(parts):
            old = jnp.where(place == 0, staged[v], late[v])
            staged[v] = jnp.where(lane_own < 3, pltpu.roll(new, LANES - 16, 1), jnp.where(lane_own >= 125, new, old))
            copy = pltpu.make_async_copy(staged.at[v], out.at[v], out_sems.at[i, v])
            copy.start()
            copies.append(copy)

    sections(fix, w0, wa, wb, coeff, table, emit)
    for copy in copies:
        copy.wait()


VMEM = pl.BlockSpec(memory_space=pltpu.VMEM)
HBM = pl.BlockSpec(memory_space=pltpu.HBM)
ANY = pl.BlockSpec(memory_space=pl.ANY)
SMEM = pl.BlockSpec(memory_space=pltpu.SMEM)
SCRATCH = [pltpu.VMEM((14, ROWS, LANES), jnp.float32)] * 3 + [pltpu.VMEM((2, ROWS, LANES), jnp.float32)]
PARAMS = pltpu.CompilerParams(vmem_limit_bytes=12 * 1024 * 1024)


def f32(*shape):
    return jax.ShapeDtypeStruct(shape, jnp.float32)


def call(kernel, outs, ins, scratch=()):
    return pl.pallas_call(
        kernel, out_shape=outs, in_specs=ins, out_specs=tuple(VMEM for _ in outs), scratch_shapes=scratch, compiler_params=PARAMS,
        cost_estimate=pl.CostEstimate(flops=1, bytes_accessed=1, transcendentals=0),
    )


def at(blk, wn):
    return blk * WN + wn


def send(x, pairs):
    return lax.ppermute(x, ("blk", "wn"), pairs)


def wrap_pairs(shift):
    return [
        (at(b, w), at(b + 1, w + shift))
        for b in range(RUN - 1, BLK - 1, RUN)
        for w in range(WN)
        if 0 <= w + shift < WN
    ]


def swap(pairs):
    return pairs + [(target, source) for source, target in pairs]


def rows_pairs(start, early):
    return swap([
        (at(b, w), at(b, w + 1)) for b in range(BLK) if (b % RUN < 2 if early else b % RUN > 1) for w in range(start, WN - 1, 2)
    ])


def columns_pairs(places):
    return [(at(b, w), at(b + 1, w)) for b in range(BLK - 1) if b % RUN in places for w in range(WN)]


FIRST = swap(columns_pairs((0,)))
FORWARD = columns_pairs(range(1, RUN - 1))
BACKWARD = [(target, source) for source, target in FORWARD]
RELAY = [(at(b, w), at(b - 1, w)) for b in range(RUN, BLK, RUN) for w in range(WN)]


def idle(*outs):
    return tuple(pl.pallas_call(idle_kernel, out_shape=outs, out_specs=tuple(HBM for _ in outs))())


def in_hbm(x):
    return pltpu.with_memory_space_constraint(x, pltpu.HBM)


def local(species, flow, heat, shear, thermal):
    strips = f32(18, LANES)
    offered = f32(20, LANES)
    rows = f32(14, 8, LANES)
    halo_shape = f32(14, 16, LANES)
    out = f32(14, OWN, LANES)
    place = lax.axis_index("blk") % RUN
    block, right, corner, corner_again, table = call(
        load_kernel,
        (out, f32(4, 8, LANES), f32(4, 8, LANES), f32(3, 8, LANES), f32(248, LANES)),
        [HBM] * 5,
        [pltpu.SMEM((2, 11, 11), jnp.float32), pltpu.SemaphoreType.DMA((5,))],
    )(
        in_hbm(species.reshape(11, OWN, LANES)),
        in_hbm(flow.reshape(2, OWN, LANES)),
        in_hbm(heat.reshape(1, OWN, LANES)),
        in_hbm(shear),
        in_hbm(thermal),
    )
    wrap_down = send(corner_again, wrap_pairs(1))
    wrap = send(right, wrap_pairs(0))
    wrap_up = send(corner, wrap_pairs(-1))

    def exchange_rows(block, early):
        second, first = call(rows_kernel, (rows, f32(84, LANES)), [VMEM])(block)
        return send(first, rows_pairs(0, early)), send(second, rows_pairs(1, early))

    def early(block, table):
        first, second = exchange_rows(block, True)
        halo, pair, lows, highs, offer = call(early_columns_kernel, (halo_shape, strips, strips, strips, offered), [VMEM] * 3)(
            first, second, block
        )
        pair = send(pair, FIRST)
        final, last = lax.cond(place == 0, main, no_main, block, halo, table)
        return halo, pair, lows, highs, offer, final, last

    def not_early(block, table):
        return idle(halo_shape, strips, strips, strips, offered, out, out)

    def main(block, halo, table):
        return tuple(call(early_main_kernel, (out, out), [VMEM] * 3, SCRATCH)(block, halo, table))

    def no_main(block, halo, table):
        return idle(out, out)

    def edges(block, lows, highs):
        first, second = exchange_rows(block, False)
        return tuple(call(late_columns_kernel, (halo_shape, strips, strips), [VMEM] * 3)(first, second, block))

    def known_edges(block, lows, highs):
        return (*idle(halo_shape), *call(keep_kernel, (strips, strips), [VMEM] * 2)(lows, highs))

    def late(block, lows, highs):
        return lax.cond(place > 1, edges, known_edges, block, lows, highs)

    def not_late(block, lows, highs):
        return idle(halo_shape, strips, strips)

    early_halo, early_pair, lows, highs, offer, early_final, early_last = lax.cond(place <= 1, early, not_early, block, table)
    relay = send(offer, RELAY)
    lows = pl.pallas_call(
        join_kernel,
        out_shape=strips,
        in_specs=[ANY] + [VMEM] * 3,
        out_specs=ANY,
        input_output_aliases={0: 0},
        cost_estimate=pl.CostEstimate(flops=1, bytes_accessed=1, transcendentals=0),
    )(lows, wrap, wrap_up, wrap_down)
    halo, lows, highs = lax.cond(place > 0, late, not_late, block, lows, highs)
    left = send(highs, FORWARD)
    right = send(lows, BACKWARD)
    halo, pair, late_final, late_last = call(
        late_main_kernel,
        (halo_shape, strips, out, out),
        [VMEM] + [HBM] * 3 + [VMEM],
        SCRATCH + [pltpu.SemaphoreType.DMA((2,))],
    )(block, in_hbm(early_halo), in_hbm(halo), in_hbm(early_pair), table)
    final, last = pl.pallas_call(
        last_kernel,
        out_shape=(out, out),
        in_specs=[VMEM] * 10 + [HBM] * 2 + [VMEM] * 2,
        out_specs=(HBM, HBM),
        scratch_shapes=SCRATCH
        + [pltpu.VMEM((14, OWN, LANES), jnp.float32)] * 2
        + [pltpu.SemaphoreType.DMA((2,)), pltpu.SemaphoreType.DMA((2, 14))],
        compiler_params=PARAMS,
        cost_estimate=pl.CostEstimate(flops=1, bytes_accessed=1, transcendentals=0),
    )(
        block, halo, pair, left, right, relay, wrap, wrap_up, wrap_down, table,
        in_hbm(early_final), in_hbm(early_last), late_final, late_last,
    )
    return final.reshape(14, 16, 2, LANES), last.reshape(14, 16, 2, LANES)


def solution(mesh):
    return jax.shard_map(
        local,
        mesh=mesh,
        in_specs=(P(None, "wn", None, "blk"), P(None, "wn", None, "blk"), P("wn", None, "blk"), P(), P()),
        out_specs=(P(None, "wn", None, "blk"), P(None, "wn", None, "blk")),
        check_vma=False,
    )
```

```python
import jax
import jax.numpy as jnp
import numpy as np
from jax import lax
from jax.experimental import pallas as pl
from jax.experimental.pallas import tpu as pltpu
from jax.sharding import PartitionSpec as P

MASSES = [28.0, 32.0, 30.0, 14.0, 16.0, 28.0, 32.0, 30.0, 14.0, 16.0, 0.00055]
STEP = 0.16
WN = 8
BLK = 96
RUN = 12
OWN = 32
ROWS = 48
LANES = 128
CHUNK = 24


def iota(shape, dim):
    return lax.broadcasted_iota(jnp.int32, shape, dim)


def set_ghost_rows(state, wn):
    sub = iota((8, LANES), 0)
    low, high = wn == 0, wn == WN - 1
    for v in range(14):
        first = state[v, 0:8]
        last = state[v, 24:32]
        above = state[v, 32:40]
        below = state[v, 40:48]
        state[v, 32:40] = jnp.where(high & (sub < 2), pltpu.roll(last, 2, 0), above)
        cut = jnp.where(sub == 6, pltpu.roll(first, 3, 0), pltpu.roll(first, 5, 0))
        state[v, 40:48] = jnp.where(low & (sub >= 6), cut, below)


def coefficients(state, coeff, table):
    for c in range(ROWS // CHUNK):
        rows = pl.ds(c * CHUNK, CHUNK)
        x = [state[r, rows] for r in range(11)]
        logs = jnp.log(state[13, rows])
        visc = cond = None
        for s in range(11):
            k = 11 * s
            dv = table[k : k + 1] * x[0]
            dc = table[k + 121 : k + 122] * x[0]
            for r in range(1, 11):
                k = 11 * s + r
                dv = dv + table[k : k + 1] * x[r]
                dc = dc + table[k + 121 : k + 122] * x[r]
            tv = x[s] * np.float32(MASSES[s] / 28.0) / dv
            tc = x[s] / dc
            visc = tv if visc is None else visc + tv
            cond = tc if cond is None else cond + tc
        coeff[0, rows] = jnp.exp(0.7 * logs) * (0.5 * visc)
        coeff[1, rows] = jnp.exp(0.5 * logs) * (0.5 * cond)


def faces(coeff):
    for index, fields in ((1, (*range(11), 13)), (0, (11, 12))):
        k = coeff[index]
        face = (k + pltpu.roll(k, ROWS - 2, 0), k + pltpu.roll(k, LANES - 1, 1))
        for v in fields:
            yield v, face


def residual(w, face):
    down, across = face
    f = down * (pltpu.roll(w, ROWS - 2, 0) - w)
    g = across * (pltpu.roll(w, LANES - 1, 1) - w)
    return (f - pltpu.roll(f, 2, 0)) + (g - pltpu.roll(g, 1, 1))


def sections(fix, w0, wa, wb, coeff, table, emit):
    fix(w0)
    coefficients(w0, coeff, table)
    for v, face in faces(coeff):
        w = w0[v]
        wa[v] = w + STEP * residual(w, face)
    fix(wa)
    coefficients(wa, coeff, table)
    for v, face in faces(coeff):
        w = wa[v]
        wb[v] = 0.75 * w0[v] + 0.25 * (w + STEP * residual(w, face))
    fix(wb)
    coefficients(wb, coeff, table)
    for v, face in faces(coeff):
        w = wb[v]
        last = residual(w, face)
        final = w0[v] * np.float32(1.0 / 3.0) + np.float32(2.0 / 3.0) * (w + STEP * last)
        emit(v, final[:OWN], last[:OWN])


def pack_columns(rows):
    missing = -rows.shape[0] % LANES
    if missing:
        rows = jnp.concatenate([rows, jnp.zeros((missing, LANES), jnp.float32)], axis=0)
    left, right = [], []
    for t in range(rows.shape[0] // LANES):
        turned = rows[t * LANES : (t + 1) * LANES].T
        left.append(turned[:8])
        right.append(turned[120:])
    return left, right


def load_kernel(species, flow, heat, shear, thermal, block, right, corner, corner_again, table, matrices, sems):
    copies = [
        pltpu.make_async_copy(source, block.at[pl.ds(low, count)], sems.at[i])
        for i, (source, low, count) in enumerate(((species, 0, 11), (flow, 11, 2), (heat, 13, 1)))
    ]
    small = [pltpu.make_async_copy(source, matrices.at[i], sems.at[3 + i]) for i, source in enumerate((shear, thermal))]
    for copy in copies + small:
        copy.start()
    for copy in small:
        copy.wait()
    for i in range(2):
        for s in range(11):
            for r in range(11):
                k = 121 * i + 11 * s + r
                table[k : k + 1] = jnp.full((1, LANES), matrices[i, s, r], jnp.float32)
    for copy in copies:
        copy.wait()
    _, rights = pack_columns(block[...].reshape(14 * OWN, LANES))
    for t in range(4):
        right[t] = rights[t]
    low, high = block[:, 0:8], block[:, 24:32]
    _, rights = pack_columns(jnp.concatenate([low, high], axis=1).reshape(14 * 16, LANES))
    for t in range(4):
        corner[t] = rights[t % 2]
    for t in range(3):
        corner_again[t] = rights[t % 2]


def rows_kernel(block, second, first):
    even = lax.axis_index("wn") % 2 == 0
    second[...] = jnp.where(even, block[:, 0:8], block[:, 24:32])
    for v in range(14):
        first[pl.ds(6 * v, 6)] = jnp.where(even, block[v, 26:32], block[v, 0:6])


def join_kernel(value, a, b, c, out):
    pass


def halo_of(first, second):
    even = lax.axis_index("wn") % 2 == 0
    zeros = jnp.zeros((2, LANES), jnp.float32)
    two = second[...]
    one = [first[pl.ds(6 * v, 6)] for v in range(14)]
    above = jnp.stack([jnp.concatenate([x, zeros], axis=0) for x in one])
    below = jnp.stack([jnp.concatenate([zeros, x], axis=0) for x in one])
    return jnp.concatenate([jnp.where(even, above, two), jnp.where(even, two, below)], axis=1)


def columns_of(block, halo):
    lefts, rights = pack_columns(block[...].reshape(14 * OWN, LANES))
    lefts_halo, rights_halo = pack_columns(halo.reshape(14 * 16, LANES))
    return lefts + lefts_halo, rights + rights_halo


def early_columns_kernel(first, second, block, halo, pair, lows, highs, offer):
    even = lax.axis_index("blk") % 2 == 0
    halo[...] = halo_of(first, second)
    lefts, rights = columns_of(block, halo[...])
    for t in range(6):
        three = pl.ds(3 * t, 3)
        pair[three] = jnp.where(even, rights[t][5:8], lefts[t][0:3])
        lows[three] = lefts[t][0:3]
        offer[three] = lefts[t][0:3]
        highs[three] = rights[t][5:8]
    offer[18:20] = jnp.zeros((2, LANES), jnp.float32)


def late_columns_kernel(first, second, block, halo, lows, highs):
    halo[...] = halo_of(first, second)
    lefts, rights = columns_of(block, halo[...])
    for t in range(6):
        three = pl.ds(3 * t, 3)
        highs[three] = rights[t][5:8]
        lows[three] = lefts[t][0:3]


def keep_kernel(early_lows, early_highs, lows, highs):
    lows[...] = early_lows[...]
    highs[...] = early_highs[...]


def gather_rows(block, halo, w0):
    for v in range(14):
        w0[v, 0:OWN] = block[v]
        w0[v, OWN:ROWS] = halo[v]


def main_sections(block, halo, table, final, last, w0, wa, wb, coeff):
    wn = lax.axis_index("wn")
    if halo is not None:
        gather_rows(block, halo, w0)

    def emit(v, f, r):
        final[v] = f
        last[v] = r

    sections(lambda ref: set_ghost_rows(ref, wn), w0, wa, wb, coeff, table, emit)


def early_main_kernel(block, halo, table, final, last, w0, wa, wb, coeff):
    main_sections(block, halo, table, final, last, w0, wa, wb, coeff)


def idle_kernel(*refs):
    pass


def late_main_kernel(block, early_halo, late_halo, early_pair, table, halo, pair, final, last, w0, wa, wb, coeff, sems):
    place = lax.axis_index("blk") % RUN

    @pl.when(place <= 1)
    def _():
        copies = [pltpu.make_async_copy(early_halo, halo, sems.at[0]), pltpu.make_async_copy(early_pair, pair, sems.at[1])]
        for copy in copies:
            copy.start()
        for copy in copies:
            copy.wait()

    @pl.when(place > 1)
    def _():
        copy = pltpu.make_async_copy(late_halo, halo, sems.at[0])
        copy.start()
        copy.wait()

    @pl.when(place != 0)
    def _():
        main_sections(block, halo, table, final, last, w0, wa, wb, coeff)


def last_kernel(
    block, halo, pair, left, right, relay, wrap, wrap_up, wrap_down, table,
    early_final, early_last, late_final, late_last, final, last, w0, wa, wb, coeff, finals, lasts, in_sems, out_sems,
):
    wn = lax.axis_index("wn")
    blk = lax.axis_index("blk")
    place = blk % RUN
    mains = [pltpu.make_async_copy(a, b, in_sems.at[i]) for i, (a, b) in enumerate(((early_final, finals), (early_last, lasts)))]

    @pl.when(place == 0)
    def _():
        for copy in mains:
            copy.start()

    lane = iota((ROWS, LANES), 1)
    gather_rows(block, halo, w0)

    lane3 = iota((3, LANES), 1)
    tiles = []
    for t in range(6):
        three = pl.ds(3 * t, 3)
        if t < 4:
            from_wrap = wrap[t, 5:8]
        else:
            from_wrap = jnp.where(lane3 % 16 < 8, wrap_up[t - 4, 5:8], wrap_down[t - 4, 5:8])
        lo = jnp.where(place == 0, from_wrap, jnp.where(place == 1, pair[three], left[three]))
        hi = jnp.where(place == RUN - 1, relay[three], jnp.where(place == 0, pair[three], right[three]))
        full = jnp.concatenate([hi, jnp.zeros((10, LANES), jnp.float32), lo, jnp.zeros((112, LANES), jnp.float32)], axis=0)
        tiles.append(full.T)
    for v in range(14):
        own = w0[v]
        q, h = v % 4, v % 8
        side = jnp.concatenate([tiles[v // 4][q * 32 : q * 32 + 32], tiles[4 + v // 8][h * 16 : h * 16 + 16]], axis=0)
        w0[v] = jnp.where(lane < 16, side, jnp.where(lane < 72, pltpu.roll(own, 16, 1), own))

    first, nose = blk == 0, blk == BLK - 1
    even_row = iota((ROWS, LANES), 0) % 2 == 0

    def fix(ref):
        set_ghost_rows(ref, wn)

        @pl.when(first)
        def _():
            for v in range(14):
                w = ref[v]
                ref[v] = jnp.where(lane == 15, pltpu.roll(w, LANES - 1, 1), w)

        @pl.when(nose)
        def _():
            for v in range(14):
                w = ref[v]
                moved = pltpu.roll(w, 1, 1)
                swapped = jnp.where(even_row, pltpu.roll(moved, ROWS - 1, 0), pltpu.roll(moved, 1, 0))
                ref[v] = jnp.where(lane == 0, swapped, w)

    lane_own = iota((OWN, LANES), 1)
    copies = []

    def emit(v, f, r):
        if v == 0:

            @pl.when(place == 0)
            def _():
                for copy in mains:
                    copy.wait()

        parts = ((final, finals, late_final, f), (last, lasts, late_last, r))
        for i, (out, staged, late, new) in enumerate(parts):
            old = jnp.where(place == 0, staged[v], late[v])
            staged[v] = jnp.where(lane_own < 3, pltpu.roll(new, LANES - 16, 1), jnp.where(lane_own >= 125, new, old))
            copy = pltpu.make_async_copy(staged.at[v], out.at[v], out_sems.at[i, v])
            copy.start()
            copies.append(copy)

    sections(fix, w0, wa, wb, coeff, table, emit)
    for copy in copies:
        copy.wait()


VMEM = pl.BlockSpec(memory_space=pltpu.VMEM)
HBM = pl.BlockSpec(memory_space=pltpu.HBM)
ANY = pl.BlockSpec(memory_space=pl.ANY)
SMEM = pl.BlockSpec(memory_space=pltpu.SMEM)
SCRATCH = [pltpu.VMEM((14, ROWS, LANES), jnp.float32)] * 3 + [pltpu.VMEM((2, ROWS, LANES), jnp.float32)]
PARAMS = pltpu.CompilerParams(vmem_limit_bytes=12 * 1024 * 1024)


def f32(*shape):
    return jax.ShapeDtypeStruct(shape, jnp.float32)


def call(kernel, outs, ins, scratch=()):
    return pl.pallas_call(
        kernel, out_shape=outs, in_specs=ins, out_specs=tuple(VMEM for _ in outs), scratch_shapes=scratch, compiler_params=PARAMS,
        cost_estimate=pl.CostEstimate(flops=1, bytes_accessed=1, transcendentals=0),
    )


def at(blk, wn):
    return blk * WN + wn


def send(x, pairs):
    return lax.ppermute(x, ("blk", "wn"), pairs)


def wrap_pairs(shift):
    return [
        (at(b, w), at(b + 1, w + shift))
        for b in range(RUN - 1, BLK - 1, RUN)
        for w in range(WN)
        if 0 <= w + shift < WN
    ]


def swap(pairs):
    return pairs + [(target, source) for source, target in pairs]


def rows_pairs(start, early):
    return swap([
        (at(b, w), at(b, w + 1)) for b in range(BLK) if (b % RUN < 2 if early else b % RUN > 1) for w in range(start, WN - 1, 2)
    ])


def columns_pairs(places):
    return [(at(b, w), at(b + 1, w)) for b in range(BLK - 1) if b % RUN in places for w in range(WN)]


FIRST = swap(columns_pairs((0,)))
FORWARD = columns_pairs(range(1, RUN - 1))
BACKWARD = [(target, source) for source, target in FORWARD]
RELAY = [(at(b, w), at(b - 1, w)) for b in range(RUN, BLK, RUN) for w in range(WN)]


def idle(*outs):
    return tuple(pl.pallas_call(idle_kernel, out_shape=outs, out_specs=tuple(HBM for _ in outs))())


def in_hbm(x):
    return pltpu.with_memory_space_constraint(x, pltpu.HBM)


def local(species, flow, heat, shear, thermal):
    strips = f32(18, LANES)
    offered = f32(20, LANES)
    rows = f32(14, 8, LANES)
    halo_shape = f32(14, 16, LANES)
    out = f32(14, OWN, LANES)
    place = lax.axis_index("blk") % RUN
    block, right, corner, corner_again, table = call(
        load_kernel,
        (out, f32(4, 8, LANES), f32(4, 8, LANES), f32(3, 8, LANES), f32(248, LANES)),
        [HBM] * 5,
        [pltpu.SMEM((2, 11, 11), jnp.float32), pltpu.SemaphoreType.DMA((5,))],
    )(
        in_hbm(species.reshape(11, OWN, LANES)),
        in_hbm(flow.reshape(2, OWN, LANES)),
        in_hbm(heat.reshape(1, OWN, LANES)),
        in_hbm(shear),
        in_hbm(thermal),
    )
    wrap_down = send(corner_again, wrap_pairs(1))
    wrap = send(right, wrap_pairs(0))
    wrap_up = send(corner, wrap_pairs(-1))

    def exchange_rows(block, early):
        second, first = call(rows_kernel, (rows, f32(84, LANES)), [VMEM])(block)
        return send(first, rows_pairs(0, early)), send(second, rows_pairs(1, early))

    def early(block, table):
        first, second = exchange_rows(block, True)
        halo, pair, lows, highs, offer = call(early_columns_kernel, (halo_shape, strips, strips, strips, offered), [VMEM] * 3)(
            first, second, block
        )
        pair = send(pair, FIRST)
        final, last = lax.cond(place == 0, main, no_main, block, halo, table)
        return halo, pair, lows, highs, offer, final, last

    def not_early(block, table):
        return idle(halo_shape, strips, strips, strips, offered, out, out)

    def main(block, halo, table):
        return tuple(call(early_main_kernel, (out, out), [VMEM] * 3, SCRATCH)(block, halo, table))

    def no_main(block, halo, table):
        return idle(out, out)

    def edges(block, lows, highs):
        first, second = exchange_rows(block, False)
        return tuple(call(late_columns_kernel, (halo_shape, strips, strips), [VMEM] * 3)(first, second, block))

    def known_edges(block, lows, highs):
        return (*idle(halo_shape), *call(keep_kernel, (strips, strips), [VMEM] * 2)(lows, highs))

    def late(block, lows, highs):
        return lax.cond(place > 1, edges, known_edges, block, lows, highs)

    def not_late(block, lows, highs):
        return idle(halo_shape, strips, strips)

    early_halo, early_pair, lows, highs, offer, early_final, early_last = lax.cond(place <= 1, early, not_early, block, table)
    relay = send(offer, RELAY)
    lows = pl.pallas_call(
        join_kernel,
        out_shape=strips,
        in_specs=[ANY] * 4,
        out_specs=ANY,
        input_output_aliases={0: 0},
        cost_estimate=pl.CostEstimate(flops=1, bytes_accessed=1, transcendentals=0),
    )(lows, *(pltpu.with_memory_space_constraint(x, pltpu.VMEM) for x in (wrap, wrap_up, wrap_down)))
    halo, lows, highs = lax.cond(place > 0, late, not_late, block, lows, highs)
    left = send(highs, FORWARD)
    right = send(lows, BACKWARD)
    halo, pair, late_final, late_last = call(
        late_main_kernel,
        (halo_shape, strips, out, out),
        [VMEM] + [HBM] * 3 + [VMEM],
        SCRATCH + [pltpu.SemaphoreType.DMA((2,))],
    )(block, in_hbm(early_halo), in_hbm(halo), in_hbm(early_pair), table)
    final, last = pl.pallas_call(
        last_kernel,
        out_shape=(out, out),
        in_specs=[VMEM] * 10 + [HBM] * 2 + [VMEM] * 2,
        out_specs=(HBM, HBM),
        scratch_shapes=SCRATCH
        + [pltpu.VMEM((14, OWN, LANES), jnp.float32)] * 2
        + [pltpu.SemaphoreType.DMA((2,)), pltpu.SemaphoreType.DMA((2, 14))],
        compiler_params=PARAMS,
        cost_estimate=pl.CostEstimate(flops=1, bytes_accessed=1, transcendentals=0),
    )(
        block, halo, pair, left, right, relay, wrap, wrap_up, wrap_down, table,
        in_hbm(early_final), in_hbm(early_last), late_final, late_last,
    )
    return final.reshape(14, 16, 2, LANES), last.reshape(14, 16, 2, LANES)


def solution(mesh):
    return jax.shard_map(
        local,
        mesh=mesh,
        in_specs=(P(None, "wn", None, "blk"), P(None, "wn", None, "blk"), P("wn", None, "blk"), P(), P()),
        out_specs=(P(None, "wn", None, "blk"), P(None, "wn", None, "blk")),
        check_vma=False,
    )
```

```python
import jax
import jax.numpy as jnp
import numpy as np
from jax import lax
from jax.experimental import pallas as pl
from jax.experimental.pallas import tpu as pltpu
from jax.sharding import PartitionSpec as P

MASSES = [28.0, 32.0, 30.0, 14.0, 16.0, 28.0, 32.0, 30.0, 14.0, 16.0, 0.00055]
STEP = 0.16
WN = 8
BLK = 96
RUN = 12
OWN = 32
ROWS = 48
LANES = 128
CHUNK = 24


def iota(shape, dim):
    return lax.broadcasted_iota(jnp.int32, shape, dim)


def set_ghost_rows(state, wn):
    sub = iota((8, LANES), 0)
    low, high = wn == 0, wn == WN - 1
    for v in range(14):
        first = state[v, 0:8]
        last = state[v, 24:32]
        above = state[v, 32:40]
        below = state[v, 40:48]
        state[v, 32:40] = jnp.where(high & (sub < 2), pltpu.roll(last, 2, 0), above)
        cut = jnp.where(sub == 6, pltpu.roll(first, 3, 0), pltpu.roll(first, 5, 0))
        state[v, 40:48] = jnp.where(low & (sub >= 6), cut, below)


def coefficients(state, coeff, table):
    for c in range(ROWS // CHUNK):
        rows = pl.ds(c * CHUNK, CHUNK)
        x = [state[r, rows] for r in range(11)]
        logs = jnp.log(state[13, rows])
        visc = cond = None
        for s in range(11):
            k = 11 * s
            dv = table[k : k + 1] * x[0]
            dc = table[k + 121 : k + 122] * x[0]
            for r in range(1, 11):
                k = 11 * s + r
                dv = dv + table[k : k + 1] * x[r]
                dc = dc + table[k + 121 : k + 122] * x[r]
            tv = x[s] * np.float32(MASSES[s] / 28.0) / dv
            tc = x[s] / dc
            visc = tv if visc is None else visc + tv
            cond = tc if cond is None else cond + tc
        coeff[0, rows] = jnp.exp(0.7 * logs) * (0.5 * visc)
        coeff[1, rows] = jnp.exp(0.5 * logs) * (0.5 * cond)


def faces(coeff):
    for index, fields in ((1, (*range(11), 13)), (0, (11, 12))):
        k = coeff[index]
        face = (k + pltpu.roll(k, ROWS - 2, 0), k + pltpu.roll(k, LANES - 1, 1))
        for v in fields:
            yield v, face


def residual(w, face):
    down, across = face
    f = down * (pltpu.roll(w, ROWS - 2, 0) - w)
    g = across * (pltpu.roll(w, LANES - 1, 1) - w)
    return (f - pltpu.roll(f, 2, 0)) + (g - pltpu.roll(g, 1, 1))


def sections(fix, w0, wa, wb, coeff, table, emit):
    fix(w0)
    coefficients(w0, coeff, table)
    for v, face in faces(coeff):
        w = w0[v]
        wa[v] = w + STEP * residual(w, face)
    fix(wa)
    coefficients(wa, coeff, table)
    for v, face in faces(coeff):
        w = wa[v]
        wb[v] = 0.75 * w0[v] + 0.25 * (w + STEP * residual(w, face))
    fix(wb)
    coefficients(wb, coeff, table)
    for v, face in faces(coeff):
        w = wb[v]
        last = residual(w, face)
        final = w0[v] * np.float32(1.0 / 3.0) + np.float32(2.0 / 3.0) * (w + STEP * last)
        emit(v, final[:OWN], last[:OWN])


def pack_columns(rows):
    missing = -rows.shape[0] % LANES
    if missing:
        rows = jnp.concatenate([rows, jnp.zeros((missing, LANES), jnp.float32)], axis=0)
    left, right = [], []
    for t in range(rows.shape[0] // LANES):
        turned = rows[t * LANES : (t + 1) * LANES].T
        left.append(turned[:8])
        right.append(turned[120:])
    return left, right


def load_kernel(species, flow, heat, shear, thermal, block, right, corner, corner_again, table, matrices, sems):
    copies = [
        pltpu.make_async_copy(source, block.at[pl.ds(low, count)], sems.at[i])
        for i, (source, low, count) in enumerate(((species, 0, 11), (flow, 11, 2), (heat, 13, 1)))
    ]
    small = [pltpu.make_async_copy(source, matrices.at[i], sems.at[3 + i]) for i, source in enumerate((shear, thermal))]
    for copy in copies + small:
        copy.start()
    for copy in small:
        copy.wait()
    for i in range(2):
        for s in range(11):
            for r in range(11):
                k = 121 * i + 11 * s + r
                table[k : k + 1] = jnp.full((1, LANES), matrices[i, s, r], jnp.float32)
    for copy in copies:
        copy.wait()
    _, rights = pack_columns(block[...].reshape(14 * OWN, LANES))
    for t in range(4):
        right[t] = rights[t]
    low, high = block[:, 0:8], block[:, 24:32]
    _, rights = pack_columns(jnp.concatenate([low, high], axis=1).reshape(14 * 16, LANES))
    for t in range(4):
        corner[t] = rights[t % 2]
    for t in range(3):
        corner_again[t] = rights[t % 2]


def rows_kernel(block, second, first):
    even = lax.axis_index("wn") % 2 == 0
    second[...] = jnp.where(even, block[:, 0:8], block[:, 24:32])
    for v in range(14):
        first[pl.ds(6 * v, 6)] = jnp.where(even, block[v, 26:32], block[v, 0:6])


def join_kernel(value, a, b, c, out):
    pass


def halo_of(first, second):
    even = lax.axis_index("wn") % 2 == 0
    zeros = jnp.zeros((2, LANES), jnp.float32)
    two = second[...]
    one = [first[pl.ds(6 * v, 6)] for v in range(14)]
    above = jnp.stack([jnp.concatenate([x, zeros], axis=0) for x in one])
    below = jnp.stack([jnp.concatenate([zeros, x], axis=0) for x in one])
    return jnp.concatenate([jnp.where(even, above, two), jnp.where(even, two, below)], axis=1)


def columns_of(block, halo):
    lefts, rights = pack_columns(block[...].reshape(14 * OWN, LANES))
    lefts_halo, rights_halo = pack_columns(halo.reshape(14 * 16, LANES))
    return lefts + lefts_halo, rights + rights_halo


def early_columns_kernel(first, second, block, halo, pair, lows, highs, offer):
    even = lax.axis_index("blk") % 2 == 0
    halo[...] = halo_of(first, second)
    lefts, rights = columns_of(block, halo[...])
    for t in range(6):
        three = pl.ds(3 * t, 3)
        pair[three] = jnp.where(even, rights[t][5:8], lefts[t][0:3])
        lows[three] = lefts[t][0:3]
        offer[three] = lefts[t][0:3]
        highs[three] = rights[t][5:8]
    offer[18:20] = jnp.zeros((2, LANES), jnp.float32)


def late_columns_kernel(first, second, block, halo, lows, highs):
    halo[...] = halo_of(first, second)
    lefts, rights = columns_of(block, halo[...])
    for t in range(6):
        three = pl.ds(3 * t, 3)
        highs[three] = rights[t][5:8]
        lows[three] = lefts[t][0:3]


def keep_kernel(early_lows, early_highs, lows, highs):
    lows[...] = early_lows[...]
    highs[...] = early_highs[...]


def gather_rows(block, halo, w0):
    for v in range(14):
        w0[v, 0:OWN] = block[v]
        w0[v, OWN:ROWS] = halo[v]


def main_sections(block, halo, table, final, last, w0, wa, wb, coeff):
    wn = lax.axis_index("wn")
    if halo is not None:
        gather_rows(block, halo, w0)

    def emit(v, f, r):
        final[v] = f
        last[v] = r

    sections(lambda ref: set_ghost_rows(ref, wn), w0, wa, wb, coeff, table, emit)


def early_main_kernel(block, halo, table, final, last, w0, wa, wb, coeff):
    main_sections(block, halo, table, final, last, w0, wa, wb, coeff)


def idle_kernel(*refs):
    pass


def late_main_kernel(block, early_halo, late_halo, early_pair, table, halo, pair, final, last, w0, wa, wb, coeff, sems):
    place = lax.axis_index("blk") % RUN

    @pl.when(place <= 1)
    def _():
        copies = [pltpu.make_async_copy(early_halo, halo, sems.at[0]), pltpu.make_async_copy(early_pair, pair, sems.at[1])]
        for copy in copies:
            copy.start()
        for v in range(14):
            w0[v, 0:OWN] = block[v]
        for copy in copies:
            copy.wait()

    @pl.when(place > 1)
    def _():
        copy = pltpu.make_async_copy(late_halo, halo, sems.at[0])
        copy.start()
        for v in range(14):
            w0[v, 0:OWN] = block[v]
        copy.wait()

    @pl.when(place != 0)
    def _():
        for v in range(14):
            w0[v, OWN:ROWS] = halo[v]
        main_sections(block, None, table, final, last, w0, wa, wb, coeff)


def last_kernel(
    block, halo, pair, left, right, relay, wrap, wrap_up, wrap_down, table,
    early_final, early_last, late_final, late_last, final, last, w0, wa, wb, coeff, finals, lasts, in_sems, out_sems,
):
    wn = lax.axis_index("wn")
    blk = lax.axis_index("blk")
    place = blk % RUN
    mains = [pltpu.make_async_copy(a, b, in_sems.at[i]) for i, (a, b) in enumerate(((early_final, finals), (early_last, lasts)))]

    @pl.when(place == 0)
    def _():
        for copy in mains:
            copy.start()

    lane = iota((ROWS, LANES), 1)
    gather_rows(block, halo, w0)

    lane3 = iota((3, LANES), 1)
    tiles = []
    for t in range(6):
        three = pl.ds(3 * t, 3)
        if t < 4:
            from_wrap = wrap[t, 5:8]
        else:
            from_wrap = jnp.where(lane3 % 16 < 8, wrap_up[t - 4, 5:8], wrap_down[t - 4, 5:8])
        lo = jnp.where(place == 0, from_wrap, jnp.where(place == 1, pair[three], left[three]))
        hi = jnp.where(place == RUN - 1, relay[three], jnp.where(place == 0, pair[three], right[three]))
        full = jnp.concatenate([hi, jnp.zeros((10, LANES), jnp.float32), lo, jnp.zeros((112, LANES), jnp.float32)], axis=0)
        tiles.append(full.T)
    for v in range(14):
        own = w0[v]
        q, h = v % 4, v % 8
        side = jnp.concatenate([tiles[v // 4][q * 32 : q * 32 + 32], tiles[4 + v // 8][h * 16 : h * 16 + 16]], axis=0)
        w0[v] = jnp.where(lane < 16, side, jnp.where(lane < 72, pltpu.roll(own, 16, 1), own))

    first, nose = blk == 0, blk == BLK - 1
    even_row = iota((ROWS, LANES), 0) % 2 == 0

    def fix(ref):
        set_ghost_rows(ref, wn)

        @pl.when(first)
        def _():
            for v in range(14):
                w = ref[v]
                ref[v] = jnp.where(lane == 15, pltpu.roll(w, LANES - 1, 1), w)

        @pl.when(nose)
        def _():
            for v in range(14):
                w = ref[v]
                moved = pltpu.roll(w, 1, 1)
                swapped = jnp.where(even_row, pltpu.roll(moved, ROWS - 1, 0), pltpu.roll(moved, 1, 0))
                ref[v] = jnp.where(lane == 0, swapped, w)

    lane_own = iota((OWN, LANES), 1)
    copies = []

    def emit(v, f, r):
        if v == 0:

            @pl.when(place == 0)
            def _():
                for copy in mains:
                    copy.wait()

        parts = ((final, finals, late_final, f), (last, lasts, late_last, r))
        for i, (out, staged, late, new) in enumerate(parts):
            old = jnp.where(place == 0, staged[v], late[v])
            staged[v] = jnp.where(lane_own < 3, pltpu.roll(new, LANES - 16, 1), jnp.where(lane_own >= 125, new, old))
            copy = pltpu.make_async_copy(staged.at[v], out.at[v], out_sems.at[i, v])
            copy.start()
            copies.append(copy)

    sections(fix, w0, wa, wb, coeff, table, emit)
    for copy in copies:
        copy.wait()


VMEM = pl.BlockSpec(memory_space=pltpu.VMEM)
HBM = pl.BlockSpec(memory_space=pltpu.HBM)
ANY = pl.BlockSpec(memory_space=pl.ANY)
SMEM = pl.BlockSpec(memory_space=pltpu.SMEM)
SCRATCH = [pltpu.VMEM((14, ROWS, LANES), jnp.float32)] * 3 + [pltpu.VMEM((2, ROWS, LANES), jnp.float32)]
PARAMS = pltpu.CompilerParams(vmem_limit_bytes=12 * 1024 * 1024)


def f32(*shape):
    return jax.ShapeDtypeStruct(shape, jnp.float32)


def call(kernel, outs, ins, scratch=()):
    return pl.pallas_call(
        kernel, out_shape=outs, in_specs=ins, out_specs=tuple(VMEM for _ in outs), scratch_shapes=scratch, compiler_params=PARAMS,
        cost_estimate=pl.CostEstimate(flops=1, bytes_accessed=1, transcendentals=0),
    )


def at(blk, wn):
    return blk * WN + wn


def send(x, pairs):
    return lax.ppermute(x, ("blk", "wn"), pairs)


def wrap_pairs(shift):
    return [
        (at(b, w), at(b + 1, w + shift))
        for b in range(RUN - 1, BLK - 1, RUN)
        for w in range(WN)
        if 0 <= w + shift < WN
    ]


def swap(pairs):
    return pairs + [(target, source) for source, target in pairs]


def rows_pairs(start, early):
    return swap([
        (at(b, w), at(b, w + 1)) for b in range(BLK) if (b % RUN < 2 if early else b % RUN > 1) for w in range(start, WN - 1, 2)
    ])


def columns_pairs(places):
    return [(at(b, w), at(b + 1, w)) for b in range(BLK - 1) if b % RUN in places for w in range(WN)]


FIRST = swap(columns_pairs((0,)))
FORWARD = columns_pairs(range(1, RUN - 1))
BACKWARD = [(target, source) for source, target in FORWARD]
RELAY = [(at(b, w), at(b - 1, w)) for b in range(RUN, BLK, RUN) for w in range(WN)]


def idle(*outs):
    return tuple(pl.pallas_call(idle_kernel, out_shape=outs, out_specs=tuple(HBM for _ in outs))())


def in_hbm(x):
    return pltpu.with_memory_space_constraint(x, pltpu.HBM)


def local(species, flow, heat, shear, thermal):
    strips = f32(18, LANES)
    offered = f32(20, LANES)
    rows = f32(14, 8, LANES)
    halo_shape = f32(14, 16, LANES)
    out = f32(14, OWN, LANES)
    place = lax.axis_index("blk") % RUN
    block, right, corner, corner_again, table = call(
        load_kernel,
        (out, f32(4, 8, LANES), f32(4, 8, LANES), f32(3, 8, LANES), f32(248, LANES)),
        [HBM] * 5,
        [pltpu.SMEM((2, 11, 11), jnp.float32), pltpu.SemaphoreType.DMA((5,))],
    )(
        in_hbm(species.reshape(11, OWN, LANES)),
        in_hbm(flow.reshape(2, OWN, LANES)),
        in_hbm(heat.reshape(1, OWN, LANES)),
        in_hbm(shear),
        in_hbm(thermal),
    )
    wrap_down = send(corner_again, wrap_pairs(1))
    wrap = send(right, wrap_pairs(0))
    wrap_up = send(corner, wrap_pairs(-1))

    def exchange_rows(block, early):
        second, first = call(rows_kernel, (rows, f32(84, LANES)), [VMEM])(block)
        return send(first, rows_pairs(0, early)), send(second, rows_pairs(1, early))

    def early(block, table):
        first, second = exchange_rows(block, True)
        halo, pair, lows, highs, offer = call(early_columns_kernel, (halo_shape, strips, strips, strips, offered), [VMEM] * 3)(
            first, second, block
        )
        pair = send(pair, FIRST)
        final, last = lax.cond(place == 0, main, no_main, block, halo, table)
        return halo, pair, lows, highs, offer, final, last

    def not_early(block, table):
        return idle(halo_shape, strips, strips, strips, offered, out, out)

    def main(block, halo, table):
        return tuple(call(early_main_kernel, (out, out), [VMEM] * 3, SCRATCH)(block, halo, table))

    def no_main(block, halo, table):
        return idle(out, out)

    def edges(block, lows, highs):
        first, second = exchange_rows(block, False)
        return tuple(call(late_columns_kernel, (halo_shape, strips, strips), [VMEM] * 3)(first, second, block))

    def known_edges(block, lows, highs):
        return (*idle(halo_shape), *call(keep_kernel, (strips, strips), [VMEM] * 2)(lows, highs))

    def late(block, lows, highs):
        return lax.cond(place > 1, edges, known_edges, block, lows, highs)

    def not_late(block, lows, highs):
        return idle(halo_shape, strips, strips)

    early_halo, early_pair, lows, highs, offer, early_final, early_last = lax.cond(place <= 1, early, not_early, block, table)
    relay = send(offer, RELAY)
    lows = pl.pallas_call(
        join_kernel,
        out_shape=strips,
        in_specs=[ANY] * 4,
        out_specs=ANY,
        input_output_aliases={0: 0},
        cost_estimate=pl.CostEstimate(flops=1, bytes_accessed=1, transcendentals=0),
    )(lows, *(pltpu.with_memory_space_constraint(x, pltpu.VMEM) for x in (wrap, wrap_up, wrap_down)))
    halo, lows, highs = lax.cond(place > 0, late, not_late, block, lows, highs)
    left = send(highs, FORWARD)
    right = send(lows, BACKWARD)
    halo, pair, late_final, late_last = call(
        late_main_kernel,
        (halo_shape, strips, out, out),
        [VMEM] + [HBM] * 3 + [VMEM],
        SCRATCH + [pltpu.SemaphoreType.DMA((2,))],
    )(block, in_hbm(early_halo), in_hbm(halo), in_hbm(early_pair), table)
    final, last = pl.pallas_call(
        last_kernel,
        out_shape=(out, out),
        in_specs=[VMEM] * 10 + [HBM] * 2 + [VMEM] * 2,
        out_specs=(HBM, HBM),
        scratch_shapes=SCRATCH
        + [pltpu.VMEM((14, OWN, LANES), jnp.float32)] * 2
        + [pltpu.SemaphoreType.DMA((2,)), pltpu.SemaphoreType.DMA((2, 14))],
        compiler_params=PARAMS,
        cost_estimate=pl.CostEstimate(flops=1, bytes_accessed=1, transcendentals=0),
    )(
        block, halo, pair, left, right, relay, wrap, wrap_up, wrap_down, table,
        in_hbm(early_final), in_hbm(early_last), late_final, late_last,
    )
    return final.reshape(14, 16, 2, LANES), last.reshape(14, 16, 2, LANES)


def solution(mesh):
    return jax.shard_map(
        local,
        mesh=mesh,
        in_specs=(P(None, "wn", None, "blk"), P(None, "wn", None, "blk"), P("wn", None, "blk"), P(), P()),
        out_specs=(P(None, "wn", None, "blk"), P(None, "wn", None, "blk")),
        check_vma=False,
    )
```
